256 devices in a mesh: gy: 32 (over z, y), gz: 8 (over x, core).
Axes of the slice: x: 4, y: 4, z: 8, core: 2. Of those that a mesh axis runs over, the one named last changes fastest.
Arguments:
- flow_field: float32 [4, 512, 128, 1024], P(None, 'gy', 'gz'), may hold values from -8 to 8
Outputs:
- coefficients: float32 [4, 512, 128, 1024], P(None, 'gy', 'gz')
The draws below stay inside these ranges and needn't reach their ends.
All inputs are finite; a program needn't handle non-finite values.
Results may differ from the reference program's by a relative error of at most 0.000075.
Values sent between devices are 32-bit elements; how exact they have to be, the bound alone decides.
No kernel may reach another device: no remote copies, remote signals or barrier semaphores. Data moves between devices by JAX's collectives and lax.ppermute only.
A program may use at most 192 MiB of HBM per device.

```python
import jax
import jax.numpy as jnp
from jax import lax

NX = 1024
LEVELS = 3
NY = 512
NZ = 128


def shard_levels(key, dims, shards, smallest, high):
    def one(axis_at, shards_of):
        draws = jax.random.uniform(jax.random.fold_in(jax.random.fold_in(key, 6), axis_at), (shards_of,), jnp.float32, smallest / len(shards), high / len(shards))
        return jnp.repeat(jnp.exp(draws), dims[axis_at] // shards_of).reshape((-1,) + (1,) * (len(dims) - axis_at - 1))

    gain = one(*shards[0])
    for cut in shards[1:]:
        gain = gain * one(*cut)
    return gain


def centred(rng, shape, deviation, reach, cuts=(), dtype=jnp.bfloat16):
    level = shard_levels(rng, shape, cuts, -0.22, 0.18) if cuts else 1.0
    result = jax.random.normal(rng, shape, jnp.float32) * deviation * level
    return jnp.minimum(jnp.maximum(result, -reach), reach).astype(dtype)


def setup_inputs(seed: int = 0) -> dict:
    streams_of = jax.random.split(jax.random.key(seed), 2)
    return {
        "flow_field": centred(streams_of[0], (4, NY, NZ, NX), 1.0, 8.0, ((1, 32), (2, 8)), jnp.float32),
    }


ALPHA = -1.586134342059924
BETA = -0.052980118572961
GAMMA = 0.882911075530934
DELTA = 0.443506852043971
KAPPA = 1.149604398860241


def lift_pair(signal, axis):
    length = signal.shape[axis]
    even_part = lax.slice_in_dim(signal, 0, length, 2, axis)
    odd_part = lax.slice_in_dim(signal, 1, length, 2, axis)
    odd_part = odd_part + ALPHA * (even_part + jnp.roll(even_part, -1, axis))
    even_part = even_part + BETA * (odd_part + jnp.roll(odd_part, 1, axis))
    odd_part = odd_part + GAMMA * (even_part + jnp.roll(even_part, -1, axis))
    even_part = even_part + DELTA * (odd_part + jnp.roll(odd_part, 1, axis))
    return even_part * KAPPA, odd_part / KAPPA


def alternate(low_band, high_band, axis):
    stacked = jnp.stack([low_band, high_band], axis + 1)
    shape = list(low_band.shape)
    shape[axis] = shape[axis] * 2
    return stacked.reshape(shape)


def transform_one(component):
    for level_index in range(LEVELS):
        stride_step = 2 ** level_index
        length = NX // stride_step
        window = component[::stride_step, ::stride_step, :length]
        low_band, high_band = lift_pair(window, 2)
        window = jnp.concatenate([low_band, high_band], 2)
        low_band, high_band = lift_pair(window, 0)
        window = alternate(low_band, high_band, 0)
        low_band, high_band = lift_pair(window, 1)
        window = alternate(low_band, high_band, 1)
        component = component.at[::stride_step, ::stride_step, :length].set(window)
    return component


def reference(flow_field):
    return lax.map(transform_one, flow_field)
```

```python
import jax
import jax.numpy as jnp
import ml_dtypes
import numpy as np
from jax import lax
from jax.experimental import pallas as pl
from jax.experimental.pallas import tpu as pltpu
from jax.sharding import PartitionSpec as P

ALPHA = -1.586134342059924
BETA = -0.052980118572961
GAMMA = 0.882911075530934
DELTA = 0.443506852043971
KAPPA = 1.149604398860241

F32 = jnp.float32
BF16 = jnp.bfloat16
ROWS = 16


def pair_matrix(length):
    cells = np.eye(length)
    even, odd = cells[0::2].copy(), cells[1::2].copy()
    odd = odd + ALPHA * (even + np.roll(even, -1, 0))
    even = even + BETA * (odd + np.roll(odd, 1, 0))
    odd = odd + GAMMA * (even + np.roll(even, -1, 0))
    even = even + DELTA * (odd + np.roll(odd, 1, 0))
    return even * KAPPA, odd / KAPPA


def alternated(length):
    low, high = pair_matrix(length)
    table = np.zeros((length, length))
    table[0::2], table[1::2] = low, high
    return table


def chain_blocks():
    count = 8
    length = count * ROWS
    first = alternated(length)
    second = alternated(length // 2) @ first[0::2]
    third = alternated(length // 4) @ second[0::2]
    result = []
    for table, per in ((first, 16), (second, 8), (third, 4)):
        here = table[4 * per : 5 * per]
        result.append({k: here[:, (4 + k) * ROWS : (5 + k) * ROWS] for k in (-2, -1, 0, 1, 2)})
    return result


def factor(block, rank):
    left, size, right = np.linalg.svd(block, full_matrices=False)
    assert np.all(size[rank:] < 1e-12)
    return left[:, :rank] * size[:rank], right[:rank]


def split_const(table):
    table = np.asarray(table, np.float64)
    high = table.astype(ml_dtypes.bfloat16)
    low = (table - high.astype(np.float64)).astype(ml_dtypes.bfloat16)
    return high, low


def stack(*parts):
    return np.concatenate(parts, 0)


def tables(nx):
    first, second, third = chain_blocks()
    eye = np.eye
    sides = (-1, 1)
    out = {}
    give0, send0, give1, send1, give2a, give2b, send2 = {}, {}, {}, {}, {}, {}, {}
    give2, send2d, give22, send22 = {}, {}, {}, {}
    for s in sides:
        give0[s], send0[s] = factor(first[s], 2)
        give1[s], send1[s] = factor(second[s], 3)
        give2a[s] = third[s] @ send1[s].T
        give2b[s], send2[s] = factor(third[s] - give2a[s] @ send1[s], 2)
        give2[s], send2d[s] = factor(third[s], 4)
        give22[s], send22[s] = factor(third[2 * s], 2)
    out["send0"] = send0

    low, high = pair_matrix(nx)
    out["tx"] = np.concatenate([low[128:256, 128:640], high[128:256, 128:640]], 0).T
    low, high = pair_matrix(nx // 2)
    tx1 = np.concatenate([low, high], 0).T
    low, high = pair_matrix(nx // 4)
    tx2 = np.concatenate([low, high], 0).T
    out["tx1"], out["tx2"] = tx1, tx2
    out["tx12"] = tx1[:, : nx // 4] @ tx2

    def planes(send):
        return np.einsum("pz,ab->paBz".replace("B", "b"), send, eye(ROWS)).reshape(-1, ROWS * ROWS)

    out["zsend"] = stack(
        *[planes(send1[s]) for s in sides],
        *[planes(send2[s]) for s in sides],
        *[planes(send22[s]) for s in sides],
    )
    out["zown"] = stack(np.kron(eye(ROWS), second[0]), np.kron(eye(ROWS), third[0]))

    def back(give):
        return np.einsum("zp,ab->azpb", give, eye(ROWS)).reshape(ROWS * give.shape[0], -1)

    out["zgive1"] = np.concatenate([back(give1[s]) for s in sides], 1)
    out["zgive2"] = np.concatenate(
        [back(give2a[s]) for s in sides] + [back(give2b[s]) for s in sides] + [back(give22[s]) for s in sides], 1
    )
    out["ychain1"] = stack(np.kron(second[0], eye(8)), *[np.kron(send1[s], eye(8)) for s in sides])
    out["ychain2"] = stack(
        np.kron(third[0], eye(4)),
        *[np.kron(send2d[s], eye(4)) for s in sides],
        *[np.kron(send22[s], eye(4)) for s in sides],
    )
    out["ygive1"] = np.concatenate([np.kron(give1[s], eye(8)) for s in sides], 1)
    out["ygive2"] = np.concatenate(
        [np.kron(give2[s], eye(4)) for s in sides] + [np.kron(give22[s], eye(4)) for s in sides], 1
    )
    own = np.concatenate([np.kron(first[0], first[0])] + [np.kron(give0[s], first[0]) for s in sides], 1)
    sends = []
    for s in sides:
        for p in range(2):
            plane = send0[s][p][None]
            sends.append(
                np.concatenate([np.kron(first[0], plane)] + [np.kron(give0[t], plane) for t in sides], 1)
            )
    out["level0"] = stack(own, *sends)
    out["zgive0"] = np.concatenate([back(give0[s]) for s in sides], 1)
    return out


def split(value):
    high = value.astype(BF16)
    low = (value - high.astype(F32)).astype(BF16)
    return high, low


def dot(a, b):
    return jnp.dot(a, b, preferred_element_type=F32)


def left(table, rows):
    return dot(table[0], rows[0]) + (dot(table[0], rows[1]) + dot(table[1], rows[0]))


def right(rows, table):
    return dot(rows[0], table[0]) + (dot(rows[0], table[1]) + dot(rows[1], table[0]))


def both(high_ref, low_ref):
    return high_ref[...], low_ref[...]


def place(table, rows):
    high, low = split(rows)
    return dot(table, high) + dot(table, low)


def even_cells(width, shape):
    row = lax.broadcasted_iota(jnp.int32, shape, 0)
    return ((row | (row // width)) & 1) == 0


def lift_x(rows, table, nx, store):
    blocks = nx // 256
    for j in range(blocks):
        window = []
        for part in rows:
            if j == 0:
                window.append(jnp.concatenate([part[:, nx - 128 :], part[:, :384]], 1))
            elif j == blocks - 1:
                window.append(jnp.concatenate([part[:, nx - 384 :], part[:, :128]], 1))
            else:
                window.append(part[:, 256 * j - 128 : 256 * j + 384])
        store(j, right(window, table))


def send_y_kernel(send0, head_ref, tail_ref, to_right_ref, to_left_ref):
    for p in range(2):
        to_right_ref[0, p] = sum(float(send0[-1][p, 12 + k]) * tail_ref[0, k] for k in range(4))
        to_left_ref[0, p] = sum(float(send0[1][p, k]) * head_ref[0, k] for k in range(3))


def lift_kernel(nx, x_ref, txh, txl, zsh, zsl, t1h, t1l, t12h, t12l, uh_ref, ul_ref, r1_ref, l1_ref, r2_ref, l2_ref):
    half = nx // 2
    quarter = nx // 4

    def store(j, value):
        for k, at in enumerate((128 * j, half + 128 * j)):
            high, low = split(value[:, 128 * k : 128 * k + 128])
            uh_ref[0, :, at : at + 128] = high
            ul_ref[0, :, at : at + 128] = low

    lift_x(split(x_ref[0]), both(txh, txl), nx, store)
    planes = split(left(both(zsh, zsl), (uh_ref[0, :, :half], ul_ref[0, :, :half])))
    near = right([v[:96] for v in planes], both(t1h, t1l))
    far = right([v[96:] for v in planes], both(t12h, t12l))
    for k, (ref, ref2) in enumerate(((r1_ref, r2_ref), (l1_ref, l2_ref))):
        ref[0, :48] = near[48 * k : 48 * k + 48]
        for p in range(2):
            lanes = slice(quarter * p, quarter * p + quarter)
            ref[0, 48:, lanes] = far[32 * k + 16 * p : 32 * k + 16 * p + 16]
            ref2[0, :, lanes] = far[64 + 32 * k + 16 * p : 64 + 32 * k + 16 * p + 16]


def own_kernel(nx, uh_ref, ul_ref, zoh, zol, t1h, t1l, t12h, t12l, a1_ref, a2_ref):
    half = nx // 2
    rows = split(left(both(zoh, zol), (uh_ref[0, :, :half], ul_ref[0, :, :half])))
    a1_ref[0] = right([v[:128] for v in rows], both(t1h, t1l))
    a2_ref[0] = right([v[128:] for v in rows], both(t12h, t12l))


def chain_kernel(
    nx, a1_ref, a2_ref, l1_ref, r1_ref, l2_ref, r2_ref,
    g1h, g1l, g2h, g2l, t2h, t2l, c1h, c1l, c2h, c2l,
    o1_ref, o2_ref, to_r_ref, to_l_ref, to_r2_ref, to_l2_ref,
):
    quarter = nx // 4
    near = split(jnp.concatenate([l1_ref[0, :48], r1_ref[0, :48]], 0))
    a1 = split(a1_ref[0] + left(both(g1h, g1l), near))
    deep = [right([v[:, :quarter] for v in near], both(t2h, t2l))]
    for ref in (l1_ref, r1_ref):
        deep += [ref[0, 48:, :quarter], ref[0, 48:, quarter:]]
    for ref in (l2_ref, r2_ref):
        deep += [ref[0, :, :quarter], ref[0, :, quarter:]]
    a2 = split(a2_ref[0] + left(both(g2h, g2l), split(jnp.concatenate(deep, 0))))
    first = left(both(c1h, c1l), a1)
    second = left(both(c2h, c2l), a2)
    o1_ref[0] = first[:64]
    o2_ref[0] = second[:16]
    for k, (ref, ref2) in enumerate(((to_r_ref, to_r2_ref), (to_l_ref, to_l2_ref))):
        ref[0, :24] = first[64 + 24 * k : 88 + 24 * k]
        ref[0, 24:, :quarter] = second[16 + 16 * k : 24 + 16 * k]
        ref[0, 24:, quarter:] = second[24 + 16 * k : 32 + 16 * k]
        ref2[0] = second[48 + 8 * k : 56 + 8 * k]


def level0_kernel(nx, uh_ref, ul_ref, l_ref, r_ref, txh, txl, mh, ml, out_ref, to_r_ref, to_l_ref, high_ref, low_ref):
    half = nx // 2
    high_ref[:256] = uh_ref[0]
    low_ref[:256] = ul_ref[0]

    def store(j, value):
        for k, at in enumerate((128 * j, half + 128 * j)):
            high, low = split(value[:, 128 * k : 128 * k + 128])
            high_ref[256:, at : at + 128] = high
            low_ref[256:, at : at + 128] = low

    halo = jnp.concatenate([l_ref[0, 0], l_ref[0, 1], r_ref[0, 0], r_ref[0, 1]], 0)
    lift_x(split(halo), both(txh, txl), nx, store)
    rows = left(both(mh, ml), both(high_ref, low_ref))
    out_ref[0] = rows[:256]
    to_r_ref[0] = rows[256:288]
    to_l_ref[0] = rows[288:]


def last_kernel(
    nx, part_ref, o1_ref, o2_ref, l0_ref, r0_ref, l1_ref, r1_ref, l2_ref, r2_ref,
    g0h, g0l, g1h, g1l, g2h, g2l, e1, e2, out_ref,
):
    half = nx // 2
    quarter = nx // 4
    halo = split(jnp.concatenate([l0_ref[0], r0_ref[0]], 0))
    rows = part_ref[0] + left(both(g0h, g0l), halo)
    near = split(jnp.concatenate([l1_ref[0, :24], r1_ref[0, :24]], 0))
    first = o1_ref[0] + left(both(g1h, g1l), near)
    deep = []
    for ref in (l1_ref, r1_ref):
        deep += [ref[0, 24:, :quarter], ref[0, 24:, quarter:]]
    deep += [l2_ref[0], r2_ref[0]]
    second = o2_ref[0] + left(both(g2h, g2l), split(jnp.concatenate(deep, 0)))
    placed = place(e2[...], second)
    inner = jnp.where(even_cells(8, (64, quarter)), placed, first[:, :quarter])
    placed = place(e1[...], jnp.concatenate([inner, first[:, quarter:]], 1))
    window = jnp.where(even_cells(ROWS, (256, half)), placed, rows[:, :half])
    out_ref[0, :, :half] = window
    out_ref[0, :, half:] = rows[:, half:]


def call(body, ins, outs, consts, flops, scratch=()):
    count = ins[0].shape[0]

    def cut(shape):
        rest = len(shape) - 1
        return pl.BlockSpec((1,) + tuple(shape[1:]), lambda c: (c,) + (0,) * rest)

    def whole(shape):
        return pl.BlockSpec(tuple(shape), lambda c: (0,) * len(shape))

    moved = sum(a.size * a.dtype.itemsize for a in ins)
    moved += sum(int(np.prod(s)) * jnp.dtype(d).itemsize for s, d in outs)
    return pl.pallas_call(
        body,
        grid=(count,),
        in_specs=[cut(a.shape) for a in ins] + [whole(a.shape) for a in consts],
        out_specs=[cut(s) for s, _ in outs],
        out_shape=[jax.ShapeDtypeStruct(s, d) for s, d in outs],
        scratch_shapes=list(scratch),
        compiler_params=pltpu.CompilerParams(vmem_limit_bytes=40 * 1024 * 1024),
        cost_estimate=pl.CostEstimate(flops=flops, bytes_accessed=moved, transcendentals=0),
    )(*ins, *consts)


def move(value, axis, step):
    count = lax.axis_size(axis)
    return lax.ppermute(value, axis, [(i, (i + step) % count) for i in range(count)])


def local(flow_field):
    comps, ny, nz, nx = flow_field.shape
    assert ny == ROWS and nz == ROWS and nx % 512 == 0
    assert lax.axis_size("gy") >= 5 and lax.axis_size("gz") >= 5
    half, quarter = nx // 2, nx // 4
    table = tables(nx)
    send0 = table.pop("send0")
    pairs = {k: [jnp.asarray(p) for p in split_const(v)] for k, v in table.items()}

    def consts(*names):
        return [p for n in names for p in pairs[n]]

    spread = []
    for width in (ROWS, ROWS // 2):
        every = np.eye(width)[:, 0::2]
        spread.append(jnp.asarray(np.kron(every, every).astype(ml_dtypes.bfloat16)))

    flat = flow_field.reshape(comps, ROWS * ROWS, nx)

    edge = (1, 4, ROWS, nx)
    y_right, y_left = pl.pallas_call(
        lambda *refs: send_y_kernel(send0, *refs),
        grid=(comps,),
        in_specs=[pl.BlockSpec(edge, lambda c: (c, 0, 0, 0)), pl.BlockSpec(edge, lambda c: (c, 3, 0, 0))],
        out_specs=[pl.BlockSpec((1, 2, ROWS, nx), lambda c: (c, 0, 0, 0))] * 2,
        out_shape=[jax.ShapeDtypeStruct((comps, 2, ROWS, nx), F32)] * 2,
        cost_estimate=pl.CostEstimate(flops=1 << 22, bytes_accessed=1 << 22, transcendentals=0),
    )(flow_field, flow_field)
    from_left0 = move(y_right, "gy", 1)
    from_right0 = move(y_left, "gy", -1)

    near = (comps, 64, half)
    far = (comps, 16, half)
    uh, ul, z_right, z_left, z_right2, z_left2 = call(
        lambda *refs: lift_kernel(nx, *refs),
        [flat],
        [((comps, 256, nx), BF16)] * 2 + [(near, F32)] * 2 + [(far, F32)] * 2,
        consts("tx", "zsend", "tx1", "tx12"),
        1 << 33,
    )
    z_from_left2 = move(z_right2, "gz", 2)
    z_from_left = move(z_right, "gz", 1)
    z_from_right = move(z_left, "gz", -1)
    z_from_right2 = move(z_left2, "gz", -2)

    a1, a2 = call(
        lambda *refs: own_kernel(nx, *refs),
        [uh, ul],
        [((comps, 128, half), F32), ((comps, 64, quarter), F32)],
        consts("zown", "tx1", "tx12"),
        1 << 32,
    )
    o1, o2, y1_right, y1_left, y2_right, y2_left = call(
        lambda *refs: chain_kernel(nx, *refs),
        [a1, a2, z_from_left, z_from_right, z_from_left2, z_from_right2],
        [((comps, 64, half), F32), ((comps, 16, quarter), F32)]
        + [((comps, 32, half), F32)] * 2
        + [((comps, 8, quarter), F32)] * 2,
        consts("zgive1", "zgive2", "tx2", "ychain1", "ychain2"),
        1 << 31,
    )
    y_from_left2 = move(y2_right, "gy", 2)
    y_from_left = move(y1_right, "gy", 1)
    y_from_right = move(y1_left, "gy", -1)
    y_from_right2 = move(y2_left, "gy", -2)

    part, z0_right, z0_left = call(
        lambda *refs: level0_kernel(nx, *refs),
        [uh, ul, from_left0, from_right0],
        [((comps, 256, nx), F32)] + [((comps, 32, nx), F32)] * 2,
        consts("tx", "level0"),
        1 << 33,
        [pltpu.VMEM((320, nx), BF16)] * 2,
    )
    z0_from_left = move(z0_right, "gz", 1)
    z0_from_right = move(z0_left, "gz", -1)

    (result,) = call(
        lambda *refs: last_kernel(nx, *refs),
        [part, o1, o2, z0_from_left, z0_from_right, y_from_left, y_from_right, y_from_left2, y_from_right2],
        [((comps, ROWS * ROWS, nx), F32)],
        consts("zgive0", "ygive1", "ygive2") + spread,
        1 << 31,
    )
    return result.reshape(flow_field.shape)


def solution(mesh):
    placed = P(None, "gy", "gz", None)
    return jax.shard_map(local, mesh=mesh, in_specs=(placed,), out_specs=placed, check_vma=False)
```

```python
import jax
import jax.numpy as jnp
import ml_dtypes
import numpy as np
from jax import lax
from jax.experimental import pallas as pl
from jax.experimental.pallas import tpu as pltpu
from jax.sharding import PartitionSpec as P

ALPHA = -1.586134342059924
BETA = -0.052980118572961
GAMMA = 0.882911075530934
DELTA = 0.443506852043971
KAPPA = 1.149604398860241

F32 = jnp.float32
BF16 = jnp.bfloat16
VMEM_LIMIT = 32 * 1024 * 1024
ROWS = 16


def pair_matrix(length):
    cells = np.eye(length)
    even, odd = cells[0::2].copy(), cells[1::2].copy()
    odd = odd + ALPHA * (even + np.roll(even, -1, 0))
    even = even + BETA * (odd + np.roll(odd, 1, 0))
    odd = odd + GAMMA * (even + np.roll(even, -1, 0))
    even = even + DELTA * (odd + np.roll(odd, 1, 0))
    return even * KAPPA, odd / KAPPA


def alternated(length):
    low, high = pair_matrix(length)
    table = np.zeros((length, length))
    table[0::2], table[1::2] = low, high
    return table


def chain_blocks():
    count = 8
    length = count * ROWS
    first = alternated(length)
    second = alternated(length // 2) @ first[0::2]
    third = alternated(length // 4) @ second[0::2]
    result = []
    for table, per in ((first, 16), (second, 8), (third, 4)):
        here = table[4 * per : 5 * per]
        result.append({k: here[:, (4 + k) * ROWS : (5 + k) * ROWS] for k in (-2, -1, 0, 1, 2)})
    return result


def factor(block, rank):
    left, size, right = np.linalg.svd(block, full_matrices=False)
    assert np.all(size[rank:] < 1e-12)
    return left[:, :rank] * size[:rank], right[:rank]


def split_const(table):
    table = np.asarray(table, np.float64)
    high = table.astype(ml_dtypes.bfloat16)
    low = (table - high.astype(np.float64)).astype(ml_dtypes.bfloat16)
    return high, low


def stack(*parts):
    return np.concatenate(parts, 0)


def tables(nx):
    first, second, third = chain_blocks()
    eye = np.eye
    sides = (-1, 1)
    out = {}
    give1, send1, give2a, give2b, send2 = {}, {}, {}, {}, {}
    give2, send2d, give22, send22 = {}, {}, {}, {}
    for s in sides:
        give1[s], send1[s] = factor(second[s], 3)
        give2a[s] = third[s] @ send1[s].T
        give2b[s], send2[s] = factor(third[s] - give2a[s] @ send1[s], 2)
        give2[s], send2d[s] = factor(third[s], 4)
        give22[s], send22[s] = factor(third[2 * s], 2)

    low, high = pair_matrix(nx)
    out["tx"] = np.concatenate([low[128:256, 256:512], high[128:256, 256:512]], 0).T
    blocks = nx // 256
    rims = np.zeros((8 * blocks, nx))
    for j in range(blocks):
        block = np.concatenate([low[128 * j : 128 * j + 128], high[128 * j : 128 * j + 128]], 0).T
        after = (j + 1) % blocks
        rims[8 * j : 8 * j + 4, 256 * j : 256 * j + 256] = block[(256 * j - np.arange(4, 0, -1)) % nx]
        rims[8 * after + 4 : 8 * after + 8, 256 * j : 256 * j + 256] = block[256 * after : 256 * after + 4]
    low, high = pair_matrix(nx // 2)
    tx1 = np.concatenate([low, high], 0).T
    low, high = pair_matrix(nx // 4)
    tx2 = np.concatenate([low, high], 0).T
    out["tx1"] = tx1
    out["tx12"] = tx1[:, : nx // 4] @ tx2

    def planes(send):
        return np.einsum("pz,ab->paBz".replace("B", "b"), send, eye(ROWS)).reshape(-1, ROWS * ROWS)

    out["zsend"] = stack(*[planes(send1[s]) for s in sides], *[planes(send2[s]) for s in sides])
    out["zown"] = stack(
        np.kron(eye(ROWS), second[0]), np.kron(eye(ROWS), third[0]), *[planes(send22[s]) for s in sides]
    )

    def back(give):
        return np.einsum("zp,ab->azpb", give, eye(ROWS)).reshape(ROWS * give.shape[0], -1)

    zgive1 = np.concatenate([back(give1[s]) for s in sides], 1)
    zgive2a = np.concatenate([back(give2a[s]) for s in sides], 1)
    zgive2b = np.concatenate([back(give2b[s]) for s in sides] + [back(give22[s]) for s in sides], 1)
    out["ychain1"] = stack(np.kron(second[0], eye(8)), *[np.kron(send1[s], eye(8)) for s in sides])
    out["ychain2"] = stack(
        np.kron(third[0], eye(4)),
        *[np.kron(send2d[s], eye(4)) for s in sides],
        *[np.kron(send22[s], eye(4)) for s in sides],
    )
    out["chain1"] = stack(out["ychain1"] @ zgive1, out["ychain2"] @ zgive2a)
    out["chain2"] = out["ychain2"] @ zgive2b
    out["ygive1"] = np.concatenate([np.kron(give1[s], eye(8)) for s in sides], 1)
    out["ygive2"] = np.concatenate(
        [np.kron(give2[s], eye(4)) for s in sides] + [np.kron(give22[s], eye(4)) for s in sides], 1
    )
    pairs = {name: split_const(table) for name, table in out.items()}
    high, low = split_const(rims)
    pairs["rims"] = (np.concatenate([high, high, low, np.zeros_like(high)], 0),)
    return pairs


def split(value):
    high = value.astype(BF16)
    low = (value - high.astype(F32)).astype(BF16)
    return high, low


def dot(a, b):
    return jnp.dot(a, b, preferred_element_type=F32)


def left(table, rows):
    return dot(table[0], rows[0]) + (dot(table[0], rows[1]) + dot(table[1], rows[0]))


def right(rows, table):
    return dot(rows[0], table[0]) + (dot(rows[0], table[1]) + dot(rows[1], table[0]))


def both(high_ref, low_ref):
    return high_ref[...], low_ref[...]


def lift_line(cells, before, after):
    even, odd = list(cells[0::2]), list(cells[1::2])
    count = len(even)
    even.append(after[0])
    odd = [odd[n] + ALPHA * (even[n] + even[n + 1]) for n in range(count)]
    odd_before = before[0] + ALPHA * even[0]
    even_before = before[1] + BETA * odd_before
    odd_around = [odd_before] + odd + [after[1]]
    even = [even[n] + BETA * (odd_around[n + 1] + odd_around[n]) for n in range(count + 1)]
    odd = [odd[n] + GAMMA * (even[n] + even[n + 1]) for n in range(count)]
    odd_around = [odd_before + GAMMA * (even_before + even[0])] + odd
    even = [even[n] + DELTA * (odd_around[n + 1] + odd_around[n]) for n in range(count)]
    result = []
    for n in range(count):
        result += [even[n] * KAPPA, odd[n] * (1.0 / KAPPA)]
    return result


def give_right(cells):
    a, b, c, d = cells
    return d + ALPHA * c, c + BETA * (b + ALPHA * (a + c))


def give_left(cells):
    a, b, c = cells
    return a, b + ALPHA * (a + c)


def lift_x(cells, table, rims_ref, store):
    count, nx = cells.shape
    lane = lax.broadcasted_iota(jnp.int32, (count, 128), 1)
    rims = None
    for j in range(nx // 256):
        at = 256 * j
        before = cells[:, nx - 128 :] if j == 0 else cells[:, at - 128 : at]
        rim = jnp.where(lane >= 124, before, jnp.where(lane < 4, cells[:, at : at + 128], 0.0))
        rim = pltpu.roll(rim, 4 + 8 * j, 1)
        rims = rim if rims is None else rims + rim
    width = nx // 32
    high = rims.astype(BF16).astype(F32)
    rims = (high + pltpu.roll(rims - high, width, 1) + pltpu.roll(high, 2 * width, 1)).astype(BF16)
    parts = split(cells)
    for j in range(nx // 256):
        lanes = slice(256 * j, 256 * j + 256)
        store(j, right([part[:, lanes] for part in parts], table) + dot(rims, rims_ref[:, lanes]))


def edge_kernel(x_ref, to_right_ref, to_left_ref, rows_ref, sems):
    comps = x_ref.shape[0]
    copies = []
    for c in range(comps):
        copies.append(pltpu.make_async_copy(x_ref.at[c, pl.ds(0, 3)], rows_ref.at[c, pl.ds(0, 3)], sems.at[c, 0]))
        copies.append(pltpu.make_async_copy(x_ref.at[c, pl.ds(12, 4)], rows_ref.at[c, pl.ds(3, 4)], sems.at[c, 1]))
    for copy in copies:
        copy.start()
    for c in range(comps):
        copies[2 * c].wait()
        to_left_ref[c, 0], to_left_ref[c, 1] = give_left([rows_ref[c, k] for k in range(3)])
        copies[2 * c + 1].wait()
        to_right_ref[c, 0], to_right_ref[c, 1] = give_right([rows_ref[c, k] for k in range(3, 7)])


def lift_kernel(
    x_ref, txh, txl, rims, zsh, zsl, t12h, t12l,
    u_ref, high_ref, low_ref, r1_ref, l1_ref, cells_ref, far_ref, sems,
):
    comps, _, nx = x_ref.shape
    blocks, quarter = nx // 256, nx // 4

    def copy(c):
        return pltpu.make_async_copy(x_ref.at[c], cells_ref.at[c], sems.at[c])

    copy(0).start()
    copy(1).start()

    def step(c, _):
        copy(c).wait()

        @pl.when(c + 2 < comps)
        def _():
            copy(c + 2).start()

        def store(j, value):
            u_ref[c, j] = value[:, :128]
            u_ref[c, blocks + j] = value[:, 128:]
            high, low = split(value[:, :128])
            high_ref[c, :, 128 * j : 128 * j + 128] = high
            low_ref[c, :, 128 * j : 128 * j + 128] = low

        lift_x(cells_ref[c], both(txh, txl), rims, store)
        rows = left(both(zsh, zsl), (high_ref[c], low_ref[c]))
        r1_ref[c, :48] = rows[:48]
        l1_ref[c, :48] = rows[48:96]
        far_ref[c] = rows[96:]
        return 0

    lax.fori_loop(0, comps, step, 0)
    far = right(split(far_ref[...].reshape(64 * comps, nx // 2)), both(t12h, t12l))
    for c in range(comps):
        for k, ref in enumerate((r1_ref, l1_ref)):
            for p in range(2):
                at = 64 * c + 32 * k + 16 * p
                ref[c, 48:, quarter * p : quarter * p + quarter] = far[at : at + 16]


def own_kernel(
    high_ref, low_ref, zoh, zol, t12h, t12l, c1h, c1l, c2h, c2l, first_ref, second_ref, r2_ref, l2_ref, far_ref
):
    comps, _, half = high_ref.shape
    quarter = half // 2

    def step(c, _):
        rows = left(both(zoh, zol), (high_ref[c], low_ref[c]))
        first_ref[c] = left(both(c1h, c1l), split(rows[:128]))
        far_ref[c] = rows[128:]
        return 0

    lax.fori_loop(0, comps, step, 0)
    far = right(split(far_ref[...].reshape(128 * comps, half)), both(t12h, t12l))
    for c in range(comps):
        second_ref[c] = left(both(c2h, c2l), split(far[128 * c : 128 * c + 64]))
        for k, ref in enumerate((r2_ref, l2_ref)):
            for p in range(2):
                at = 128 * c + 64 + 32 * k + 16 * p
                ref[c, :, quarter * p : quarter * p + quarter] = far[at : at + 16]


def chain_kernel(
    first_ref, second_ref, l1_ref, r1_ref, l2_ref, r2_ref,
    g1h, g1l, g2h, g2l, t12h, t12l,
    o1_ref, o2_ref, to_r_ref, to_l_ref, to_r2_ref, to_l2_ref, far_ref,
):
    comps, _, half = first_ref.shape
    quarter = half // 2

    def step(c, _):
        near = split(jnp.concatenate([l1_ref[c, :48], r1_ref[c, :48]], 0))
        rows = left(both(g1h, g1l), near)
        far_ref[c] = rows[112:]
        first = first_ref[c] + rows[:112]
        o1_ref[c] = first[:64]
        to_r_ref[c, :24] = first[64:88]
        to_l_ref[c, :24] = first[88:]
        return 0

    lax.fori_loop(0, comps, step, 0)
    far = right(split(far_ref[...].reshape(64 * comps, half)), both(t12h, t12l))
    for c in range(comps):
        deep = []
        for ref in (l1_ref, r1_ref):
            deep += [ref[c, 48:, :quarter], ref[c, 48:, quarter:]]
        for ref in (l2_ref, r2_ref):
            deep += [ref[c, :, :quarter], ref[c, :, quarter:]]
        second = left(both(g2h, g2l), split(jnp.concatenate(deep, 0)))
        second = second_ref[c] + (far[64 * c : 64 * c + 64] + second)
        o2_ref[c] = second[:16]
        for k, (ref, ref2) in enumerate(((to_r_ref, to_r2_ref), (to_l_ref, to_l2_ref))):
            ref[c, 24:, :quarter] = second[16 + 16 * k : 24 + 16 * k]
            ref[c, 24:, quarter:] = second[24 + 16 * k : 32 + 16 * k]
            ref2[c] = second[48 + 8 * k : 56 + 8 * k]


def along_y_kernel(u_ref, l_ref, r_ref, txh, txl, rims, b_ref, to_r_ref, to_l_ref, halo_ref):
    comps, lanes = u_ref.shape[:2]
    blocks = lanes // 2

    def store(j, value):
        halo_ref[j] = value[:, :128]
        halo_ref[blocks + j] = value[:, 128:]

    rows = [ref[c, p] for c in range(comps) for ref in (l_ref, r_ref) for p in range(2)]
    lift_x(jnp.concatenate(rows, 0), both(txh, txl), rims, store)

    def step(n, _):
        c, k = n // lanes, n % lanes
        u, b, halo = u_ref.at[c, k], b_ref.at[c, k], halo_ref.at[k]
        for part in range(2):
            cells = [u[16 * y + 8 * part : 16 * y + 8 * part + 8] for y in range(ROWS)]
            around = [halo[pl.ds(pl.multiple_of(64 * c + 16 * p + 8 * part, 8), 8)] for p in range(4)]
            for y, value in enumerate(lift_line(cells, around[:2], around[2:])):
                b[pl.ds(128 * part + y, 8, stride=ROWS)] = value

        def plane(z):
            return b[16 * z : 16 * z + 16]

        to_r_ref[c, k, 0], to_r_ref[c, k, 1] = give_right([plane(z) for z in range(12, 16)])
        to_l_ref[c, k, 0], to_l_ref[c, k, 1] = give_left([plane(z) for z in range(3)])
        return 0

    lax.fori_loop(0, comps * lanes, step, 0)


def along_z_kernel(b_ref, l_ref, r_ref, out_ref, even_ref, done_ref, sems):
    comps, lanes = b_ref.shape[:2]

    def copy(c, k):
        return pltpu.make_async_copy(
            done_ref.at[c, k], out_ref.at[c, :, pl.ds(pl.multiple_of(128 * k, 128), 128)], sems.at[c]
        )

    def step(n, _):
        c, k = n // lanes, n % lanes
        b, done = b_ref.at[c, k], done_ref.at[c, k]
        for part in range(2):
            cells = [b[16 * z + 8 * part : 16 * z + 8 * part + 8] for z in range(ROWS)]
            around = [ref[c, k, p, 8 * part : 8 * part + 8] for ref in (l_ref, r_ref) for p in range(2)]
            for z, value in enumerate(lift_line(cells, around[:2], around[2:])):
                done[pl.ds(128 * part + z, 8, stride=ROWS)] = value
        copy(c, k).start()

        @pl.when(k < lanes // 2)
        def _():
            for y in range(ROWS // 2):
                even_ref[c, k, 16 * y : 16 * y + 16] = done[32 * y : 32 * y + 16]

        return 0

    lax.fori_loop(0, comps * lanes, step, 0)
    for c in range(comps):
        for k in range(lanes):
            copy(c, k).wait()


def last_kernel(
    _, even_ref, o1_ref, o2_ref, l1_ref, r1_ref, l2_ref, r2_ref,
    g1h, g1l, g2h, g2l, t1h, t1l, out_ref, done_ref, sems,
):
    comps, lanes = even_ref.shape[:2]
    half = 128 * lanes
    quarter = half // 2
    window, deepest = [], []
    for c in range(comps):
        near = split(jnp.concatenate([l1_ref[c, :24], r1_ref[c, :24]], 0))
        window.append(o1_ref[c] + left(both(g1h, g1l), near))
        deep = []
        for ref in (l1_ref, r1_ref):
            deep += [ref[c, 24:, :quarter], ref[c, 24:, quarter:]]
        deep += [l2_ref[c], r2_ref[c]]
        deepest.append(o2_ref[c] + left(both(g2h, g2l), split(jnp.concatenate(deep, 0))))
    window = right(split(jnp.concatenate(window, 0)), both(t1h, t1l))
    copies = []
    for c in range(comps):
        for k in range(lanes):
            at = slice(128 * k, 128 * k + 128)
            done = done_ref.at[c, k]
            done[...] = even_ref[c, k]
            for y in range(8):
                done[pl.ds(16 * y, 8, stride=2)] = window[64 * c + 8 * y : 64 * c + 8 * y + 8, at]
            if 128 * k < quarter:
                for y in range(4):
                    done[pl.ds(32 * y, 4, stride=4)] = deepest[c][4 * y : 4 * y + 4, at]
            for y in range(8):
                copies.append(
                    pltpu.make_async_copy(done.at[pl.ds(16 * y, 16)], out_ref.at[c, pl.ds(32 * y, 16), at], sems.at[c])
                )
                copies[-1].start()
    for copy in copies:
        copy.wait()


def call(body, ins, outs, scratch=(), flops=0, hbm_in=(), hbm_out=(), aliases=None):
    def spec(n, hbm):
        return pl.BlockSpec(memory_space=pltpu.HBM if n in hbm else pltpu.VMEM)

    moved = sum(a.size * a.dtype.itemsize for a in ins)
    moved += sum(int(np.prod(s)) * jnp.dtype(d).itemsize for s, d in outs)
    return pl.pallas_call(
        body,
        in_specs=[spec(n, hbm_in) for n in range(len(ins))],
        out_specs=[spec(n, hbm_out) for n in range(len(outs))],
        out_shape=[jax.ShapeDtypeStruct(s, d) for s, d in outs],
        scratch_shapes=list(scratch),
        input_output_aliases=aliases or {},
        compiler_params=pltpu.CompilerParams(vmem_limit_bytes=VMEM_LIMIT),
        cost_estimate=pl.CostEstimate(flops=flops, bytes_accessed=moved, transcendentals=0),
    )(*ins)


def move(value, axis, step):
    count = lax.axis_size(axis)
    return lax.ppermute(value, axis, [(i, (i + step) % count) for i in range(count)])


def local(flow_field):
    comps, ny, nz, nx = flow_field.shape
    assert ny == ROWS and nz == ROWS and nx % 1024 == 0
    assert lax.axis_size("gy") >= 5 and lax.axis_size("gz") >= 5
    half, quarter, lanes = nx // 2, nx // 4, nx // 128
    pairs = {k: [jnp.asarray(p) for p in v] for k, v in tables(nx).items()}
    field = pltpu.with_memory_space_constraint(flow_field, pltpu.HBM)
    flat = pltpu.with_memory_space_constraint(flow_field.reshape(comps, ROWS * ROWS, nx), pltpu.HBM)

    def consts(*names):
        return [p for n in names for p in pairs[n]]

    def dma(*shape):
        return pltpu.SemaphoreType.DMA(shape)

    edge = ((comps, 2, ROWS, nx), F32)
    y_right, y_left = call(
        edge_kernel,
        [field],
        [edge] * 2,
        [pltpu.VMEM((comps, 7, ROWS, nx), F32), dma(comps, 2)],
        hbm_in=(0,),
    )
    from_left0 = move(y_right, "gy", 1)
    from_right0 = move(y_left, "gy", -1)

    near = ((comps, 64, half), F32)
    far = ((comps, 16, half), F32)
    cells = ((comps, lanes, ROWS * ROWS, 128), F32)
    u, high, low, z_right, z_left = call(
        lift_kernel,
        [flat] + consts("tx", "rims", "zsend", "tx12"),
        [cells] + [((comps, ROWS * ROWS, half), BF16)] * 2 + [near] * 2,
        [pltpu.VMEM((comps, ROWS * ROWS, nx), F32), pltpu.VMEM((comps, 64, half), F32), dma(comps)],
        flops=1 << 33,
        hbm_in=(0,),
    )
    z_from_left = move(z_right, "gz", 1)
    z_from_right = move(z_left, "gz", -1)

    first, second, z_right2, z_left2 = call(
        own_kernel,
        [high, low] + consts("zown", "tx12", "ychain1", "ychain2"),
        [((comps, 112, half), F32), ((comps, 64, quarter), F32)] + [far] * 2,
        [pltpu.VMEM((comps, 128, half), F32)],
        flops=1 << 32,
    )
    z_from_left2 = move(z_right2, "gz", 2)
    z_from_right2 = move(z_left2, "gz", -2)

    planes = ((comps, lanes, 2, ROWS, 128), F32)
    b, z0_right, z0_left = call(
        along_y_kernel,
        [u, from_left0, from_right0] + consts("tx", "rims"),
        [cells] + [planes] * 2,
        [pltpu.VMEM((lanes, 64 * comps, 128), F32)],
        flops=1 << 32,
    )
    z0_from_left = move(z0_right, "gz", 1)
    z0_from_right = move(z0_left, "gz", -1)

    o1, o2, y1_right, y1_left, y2_right, y2_left = call(
        chain_kernel,
        [first, second, z_from_left, z_from_right, z_from_left2, z_from_right2] + consts("chain1", "chain2", "tx12"),
        [((comps, 64, half), F32), ((comps, 16, quarter), F32)]
        + [((comps, 32, half), F32)] * 2
        + [((comps, 8, quarter), F32)] * 2,
        [pltpu.VMEM((comps, 64, half), F32)],
        flops=1 << 31,
    )
    y_from_left2 = move(y2_right, "gy", 2)
    y_from_left = move(y1_right, "gy", 1)
    y_from_right = move(y1_left, "gy", -1)
    y_from_right2 = move(y2_left, "gy", -2)

    whole = ((comps, ROWS * ROWS, nx), F32)
    result, even = call(
        along_z_kernel,
        [b, z0_from_left, z0_from_right],
        [whole, ((comps, lanes // 2, ROWS * ROWS // 2, 128), F32)],
        [pltpu.VMEM((comps, lanes, ROWS * ROWS, 128), F32), dma(comps)],
        flops=1 << 32,
        hbm_out=(0,),
    )
    (result,) = call(
        last_kernel,
        [result, even, o1, o2, y_from_left, y_from_right, y_from_left2, y_from_right2]
        + consts("ygive1", "ygive2", "tx1"),
        [whole],
        [pltpu.VMEM((comps, lanes // 2, ROWS * ROWS // 2, 128), F32), dma(comps)],
        flops=1 << 30,
        hbm_in=(0,),
        hbm_out=(0,),
        aliases={0: 0},
    )
    return result.reshape(flow_field.shape)


def solution(mesh):
    placed = P(None, "gy", "gz", None)
    return jax.shard_map(local, mesh=mesh, in_specs=(placed,), out_specs=placed, check_vma=False)
```

```python
import jax
import jax.numpy as jnp
import ml_dtypes
import numpy as np
from jax import lax
from jax.experimental import pallas as pl
from jax.experimental.pallas import tpu as pltpu
from jax.sharding import PartitionSpec as P

ALPHA = -1.586134342059924
BETA = -0.052980118572961
GAMMA = 0.882911075530934
DELTA = 0.443506852043971
KAPPA = 1.149604398860241

F32 = jnp.float32
BF16 = jnp.bfloat16
VMEM_LIMIT = 32 * 1024 * 1024
ROWS = 16


def pair_matrix(length):
    cells = np.eye(length)
    even, odd = cells[0::2].copy(), cells[1::2].copy()
    odd = odd + ALPHA * (even + np.roll(even, -1, 0))
    even = even + BETA * (odd + np.roll(odd, 1, 0))
    odd = odd + GAMMA * (even + np.roll(even, -1, 0))
    even = even + DELTA * (odd + np.roll(odd, 1, 0))
    return even * KAPPA, odd / KAPPA


def alternated(length):
    low, high = pair_matrix(length)
    table = np.zeros((length, length))
    table[0::2], table[1::2] = low, high
    return table


def chain_blocks():
    count = 8
    length = count * ROWS
    first = alternated(length)
    second = alternated(length // 2) @ first[0::2]
    third = alternated(length // 4) @ second[0::2]
    result = []
    for table, per in ((first, 16), (second, 8), (third, 4)):
        here = table[4 * per : 5 * per]
        result.append({k: here[:, (4 + k) * ROWS : (5 + k) * ROWS] for k in (-2, -1, 0, 1, 2)})
    return result


def factor(block, rank):
    left, size, right = np.linalg.svd(block, full_matrices=False)
    assert np.all(size[rank:] < 1e-12)
    return left[:, :rank] * size[:rank], right[:rank]


def split_const(table):
    table = np.asarray(table, np.float64)
    high = table.astype(ml_dtypes.bfloat16)
    low = (table - high.astype(np.float64)).astype(ml_dtypes.bfloat16)
    return high, low


def stack(*parts):
    return np.concatenate(parts, 0)


def tables(nx):
    first, second, third = chain_blocks()
    eye = np.eye
    sides = (-1, 1)
    out = {}
    give1, send1, give2a, give2b, send2 = {}, {}, {}, {}, {}
    give2, send2d, give22, send22 = {}, {}, {}, {}
    for s in sides:
        give1[s], send1[s] = factor(second[s], 3)
        give2a[s] = third[s] @ send1[s].T
        give2b[s], send2[s] = factor(third[s] - give2a[s] @ send1[s], 2)
        give2[s], send2d[s] = factor(third[s], 4)
        give22[s], send22[s] = factor(third[2 * s], 2)

    low, high = pair_matrix(nx)
    out["tx"] = np.concatenate([low[128:256, 256:512], high[128:256, 256:512]], 0).T
    blocks = nx // 256
    rims = np.zeros((8 * blocks, nx))
    for j in range(blocks):
        block = np.concatenate([low[128 * j : 128 * j + 128], high[128 * j : 128 * j + 128]], 0).T
        after = (j + 1) % blocks
        rims[8 * j : 8 * j + 4, 256 * j : 256 * j + 256] = block[(256 * j - np.arange(4, 0, -1)) % nx]
        rims[8 * after + 4 : 8 * after + 8, 256 * j : 256 * j + 256] = block[256 * after : 256 * after + 4]
    low, high = pair_matrix(nx // 2)
    tx1 = np.concatenate([low, high], 0).T
    low, high = pair_matrix(nx // 4)
    tx2 = np.concatenate([low, high], 0).T
    out["tx1"] = tx1
    out["tx12"] = tx1[:, : nx // 4] @ tx2

    def planes(send):
        return np.einsum("pz,ab->paBz".replace("B", "b"), send, eye(ROWS)).reshape(-1, ROWS * ROWS)

    out["zsend"] = stack(*[planes(send[s]) for send in (send1, send2, send22) for s in sides])
    out["zown"] = stack(np.kron(eye(ROWS), second[0]), np.kron(eye(ROWS), third[0]))

    def back(give):
        return np.einsum("zp,ab->azpb", give, eye(ROWS)).reshape(ROWS * give.shape[0], -1)

    zgive1 = np.concatenate([back(give1[s]) for s in sides], 1)
    zgive2a = np.concatenate([back(give2a[s]) for s in sides], 1)
    zgive2b = np.concatenate([back(give2b[s]) for s in sides] + [back(give22[s]) for s in sides], 1)
    out["ychain1"] = stack(np.kron(second[0], eye(8)), *[np.kron(send1[s], eye(8)) for s in sides])
    out["ychain2"] = stack(
        np.kron(third[0], eye(4)),
        *[np.kron(send2d[s], eye(4)) for s in sides],
        *[np.kron(send22[s], eye(4)) for s in sides],
    )
    out["chain1"] = stack(out["ychain1"] @ zgive1, out["ychain2"] @ zgive2a)
    out["chain2"] = out["ychain2"] @ zgive2b
    out["ygive1"] = np.concatenate([np.kron(give1[s], eye(8)) for s in sides], 1)
    out["ygive2"] = np.concatenate(
        [np.kron(give2[s], eye(4)) for s in sides] + [np.kron(give22[s], eye(4)) for s in sides], 1
    )
    pairs = {name: split_const(table) for name, table in out.items()}
    high, low = split_const(rims)
    pairs["rims"] = (np.concatenate([high, high, low, np.zeros_like(high)], 0),)
    return pairs


def split(value):
    high = value.astype(BF16)
    low = (value - high.astype(F32)).astype(BF16)
    return high, low


def dot(a, b):
    return jnp.dot(a, b, preferred_element_type=F32)


def left(table, rows):
    return dot(table[0], rows[0]) + (dot(table[0], rows[1]) + dot(table[1], rows[0]))


def right(rows, table):
    return dot(rows[0], table[0]) + (dot(rows[0], table[1]) + dot(rows[1], table[0]))


def both(high_ref, low_ref):
    return high_ref[...], low_ref[...]


def lift_line(cells, before, after):
    even, odd = list(cells[0::2]), list(cells[1::2])
    count = len(even)
    even.append(after[0])
    odd = [odd[n] + ALPHA * (even[n] + even[n + 1]) for n in range(count)]
    odd_before = before[0] + ALPHA * even[0]
    even_before = before[1] + BETA * odd_before
    odd_around = [odd_before] + odd + [after[1]]
    even = [even[n] + BETA * (odd_around[n + 1] + odd_around[n]) for n in range(count + 1)]
    odd = [odd[n] + GAMMA * (even[n] + even[n + 1]) for n in range(count)]
    odd_around = [odd_before + GAMMA * (even_before + even[0])] + odd
    even = [even[n] + DELTA * (odd_around[n + 1] + odd_around[n]) for n in range(count)]
    result = []
    for n in range(count):
        result += [even[n] * KAPPA, odd[n] * (1.0 / KAPPA)]
    return result


def give_right(cells):
    a, b, c, d = cells
    return d + ALPHA * c, c + BETA * (b + ALPHA * (a + c))


def give_left(cells):
    a, b, c = cells
    return a, b + ALPHA * (a + c)


def lift_x(cells, table, rims_ref, store):
    count, nx = cells.shape
    lane = lax.broadcasted_iota(jnp.int32, (count, 128), 1)
    rims = None
    for j in range(nx // 256):
        at = 256 * j
        before = cells[:, nx - 128 :] if j == 0 else cells[:, at - 128 : at]
        rim = jnp.where(lane >= 124, before, jnp.where(lane < 4, cells[:, at : at + 128], 0.0))
        rim = pltpu.roll(rim, 4 + 8 * j, 1)
        rims = rim if rims is None else rims + rim
    width = nx // 32
    high = rims.astype(BF16).astype(F32)
    rims = (high + pltpu.roll(rims - high, width, 1) + pltpu.roll(high, 2 * width, 1)).astype(BF16)
    parts = split(cells)
    for j in range(nx // 256):
        lanes = slice(256 * j, 256 * j + 256)
        store(j, right([part[:, lanes] for part in parts], table) + dot(rims, rims_ref[:, lanes]))


def edge_kernel(x_ref, to_right_ref, to_left_ref, rows_ref, sems):
    comps = x_ref.shape[0]
    copies = []
    for c in range(comps):
        copies.append(pltpu.make_async_copy(x_ref.at[c, pl.ds(0, 3)], rows_ref.at[c, pl.ds(0, 3)], sems.at[c, 0]))
        copies.append(pltpu.make_async_copy(x_ref.at[c, pl.ds(12, 4)], rows_ref.at[c, pl.ds(3, 4)], sems.at[c, 1]))
    for copy in copies:
        copy.start()
    for c in range(comps):
        copies[2 * c].wait()
        to_left_ref[c, 0], to_left_ref[c, 1] = give_left([rows_ref[c, k] for k in range(3)])
        copies[2 * c + 1].wait()
        to_right_ref[c, 0], to_right_ref[c, 1] = give_right([rows_ref[c, k] for k in range(3, 7)])


def lift_kernel(
    x_ref, txh, txl, rims, zsh, zsl, t12h, t12l,
    u_ref, high_ref, low_ref, r1_ref, l1_ref, r2_ref, l2_ref, cells_ref, far_ref, sems,
):
    comps, _, nx = x_ref.shape
    blocks, quarter = nx // 256, nx // 4

    def copy(c):
        return pltpu.make_async_copy(x_ref.at[c], cells_ref.at[c], sems.at[c])

    copy(0).start()
    copy(1).start()

    def step(c, _):
        copy(c).wait()

        @pl.when(c + 2 < comps)
        def _():
            copy(c + 2).start()

        def store(j, value):
            u_ref[c, j] = value[:, :128]
            u_ref[c, blocks + j] = value[:, 128:]
            high, low = split(value[:, :128])
            high_ref[c, :, 128 * j : 128 * j + 128] = high
            low_ref[c, :, 128 * j : 128 * j + 128] = low

        lift_x(cells_ref[c], both(txh, txl), rims, store)
        rows = left(both(zsh, zsl), (high_ref[c], low_ref[c]))
        r1_ref[c, :48] = rows[:48]
        l1_ref[c, :48] = rows[48:96]
        far_ref[c] = rows[96:]
        return 0

    lax.fori_loop(0, comps, step, 0)
    far = right(split(far_ref[...].reshape(128 * comps, nx // 2)), both(t12h, t12l))
    for c in range(comps):
        for k, (ref, ref2) in enumerate(((r1_ref, r2_ref), (l1_ref, l2_ref))):
            for p in range(2):
                lanes = slice(quarter * p, quarter * p + quarter)
                at = 128 * c + 32 * k + 16 * p
                ref[c, 48:, lanes] = far[at : at + 16]
                ref2[c, :, lanes] = far[at + 64 : at + 80]


def own_kernel(
    high_ref, low_ref, zoh, zol, t12h, t12l, c1h, c1l, c2h, c2l, first_ref, second_ref, token_ref, far_ref,
):
    comps, _, half = high_ref.shape
    token_ref[...] = jnp.zeros_like(token_ref)

    def step(c, _):
        rows = left(both(zoh, zol), (high_ref[c], low_ref[c]))
        first_ref[c] = left(both(c1h, c1l), split(rows[:128]))
        far_ref[c] = rows[128:]
        return 0

    lax.fori_loop(0, comps, step, 0)
    far = right(split(far_ref[...].reshape(64 * comps, half)), both(t12h, t12l))
    for c in range(comps):
        second_ref[c] = left(both(c2h, c2l), split(far[64 * c : 64 * c + 64]))


def chain_kernel(
    first_ref, second_ref, l1_ref, r1_ref, l2_ref, r2_ref,
    g1h, g1l, g2h, g2l, t12h, t12l,
    o1_ref, o2_ref, to_r_ref, to_l_ref, to_r2_ref, to_l2_ref, far_ref,
):
    comps, _, half = first_ref.shape
    quarter = half // 2

    def step(c, _):
        near = split(jnp.concatenate([l1_ref[c, :48], r1_ref[c, :48]], 0))
        rows = left(both(g1h, g1l), near)
        far_ref[c] = rows[112:]
        first = first_ref[c] + rows[:112]
        o1_ref[c] = first[:64]
        to_r_ref[c, :24] = first[64:88]
        to_l_ref[c, :24] = first[88:]
        return 0

    lax.fori_loop(0, comps, step, 0)
    far = right(split(far_ref[...].reshape(64 * comps, half)), both(t12h, t12l))
    for c in range(comps):
        deep = []
        for ref in (l1_ref, r1_ref):
            deep += [ref[c, 48:, :quarter], ref[c, 48:, quarter:]]
        for ref in (l2_ref, r2_ref):
            deep += [ref[c, :, :quarter], ref[c, :, quarter:]]
        second = left(both(g2h, g2l), split(jnp.concatenate(deep, 0)))
        second = second_ref[c] + (far[64 * c : 64 * c + 64] + second)
        o2_ref[c] = second[:16]
        for k, (ref, ref2) in enumerate(((to_r_ref, to_r2_ref), (to_l_ref, to_l2_ref))):
            ref[c, 24:, :quarter] = second[16 + 16 * k : 24 + 16 * k]
            ref[c, 24:, quarter:] = second[24 + 16 * k : 32 + 16 * k]
            ref2[c] = second[48 + 8 * k : 56 + 8 * k]


def along_y_kernel(_, _2, _3, u_ref, l_ref, r_ref, txh, txl, rims, b_ref, to_r_ref, to_l_ref, halo_ref):
    comps, lanes = u_ref.shape[:2]
    blocks = lanes // 2

    def store(j, value):
        halo_ref[j] = value[:, :128]
        halo_ref[blocks + j] = value[:, 128:]

    rows = [ref[c, p] for c in range(comps) for ref in (l_ref, r_ref) for p in range(2)]
    lift_x(jnp.concatenate(rows, 0), both(txh, txl), rims, store)

    def step(n, _):
        c, k = n // lanes, n % lanes
        u, b, halo = u_ref.at[c, k], b_ref.at[c, k], halo_ref.at[k]
        for part in range(2):
            cells = [u[16 * y + 8 * part : 16 * y + 8 * part + 8] for y in range(ROWS)]
            around = [halo[pl.ds(pl.multiple_of(64 * c + 16 * p + 8 * part, 8), 8)] for p in range(4)]
            for y, value in enumerate(lift_line(cells, around[:2], around[2:])):
                b[pl.ds(128 * part + y, 8, stride=ROWS)] = value

        def plane(z):
            return b[16 * z : 16 * z + 16]

        to_r_ref[c, k, 0], to_r_ref[c, k, 1] = give_right([plane(z) for z in range(12, 16)])
        to_l_ref[c, k, 0], to_l_ref[c, k, 1] = give_left([plane(z) for z in range(3)])
        return 0

    lax.fori_loop(0, comps * lanes, step, 0)


def along_z_kernel(b_ref, l_ref, r_ref, out_ref, even_ref, done_ref, sems):
    comps, lanes = b_ref.shape[:2]

    def copy(c, k):
        return pltpu.make_async_copy(
            done_ref.at[c, k], out_ref.at[c, :, pl.ds(pl.multiple_of(128 * k, 128), 128)], sems.at[c]
        )

    def step(n, _):
        c, k = n // lanes, n % lanes
        b, done = b_ref.at[c, k], done_ref.at[c, k]
        for part in range(2):
            cells = [b[16 * z + 8 * part : 16 * z + 8 * part + 8] for z in range(ROWS)]
            around = [ref[c, k, p, 8 * part : 8 * part + 8] for ref in (l_ref, r_ref) for p in range(2)]
            for z, value in enumerate(lift_line(cells, around[:2], around[2:])):
                done[pl.ds(128 * part + z, 8, stride=ROWS)] = value
        copy(c, k).start()

        @pl.when(k < lanes // 2)
        def _():
            for y in range(ROWS // 2):
                even_ref[c, k, 16 * y : 16 * y + 16] = done[32 * y : 32 * y + 16]

        return 0

    lax.fori_loop(0, comps * lanes, step, 0)
    for c in range(comps):
        for k in range(lanes):
            copy(c, k).wait()


def last_kernel(
    _, even_ref, o1_ref, o2_ref, l1_ref, r1_ref, l2_ref, r2_ref,
    g1h, g1l, g2h, g2l, t1h, t1l, out_ref, done_ref, sems,
):
    comps, lanes = even_ref.shape[:2]
    half = 128 * lanes
    quarter = half // 2
    window, deepest = [], []
    for c in range(comps):
        near = split(jnp.concatenate([l1_ref[c, :24], r1_ref[c, :24]], 0))
        window.append(o1_ref[c] + left(both(g1h, g1l), near))
        deep = []
        for ref in (l1_ref, r1_ref):
            deep += [ref[c, 24:, :quarter], ref[c, 24:, quarter:]]
        deep += [l2_ref[c], r2_ref[c]]
        deepest.append(o2_ref[c] + left(both(g2h, g2l), split(jnp.concatenate(deep, 0))))
    window = right(split(jnp.concatenate(window, 0)), both(t1h, t1l))
    copies = []
    for c in range(comps):
        for k in range(lanes):
            at = slice(128 * k, 128 * k + 128)
            done = done_ref.at[c, k]
            done[...] = even_ref[c, k]
            for y in range(8):
                done[pl.ds(16 * y, 8, stride=2)] = window[64 * c + 8 * y : 64 * c + 8 * y + 8, at]
            if 128 * k < quarter:
                for y in range(4):
                    done[pl.ds(32 * y, 4, stride=4)] = deepest[c][4 * y : 4 * y + 4, at]
            for y in range(8):
                copies.append(
                    pltpu.make_async_copy(done.at[pl.ds(16 * y, 16)], out_ref.at[c, pl.ds(32 * y, 16), at], sems.at[c])
                )
                copies[-1].start()
    for copy in copies:
        copy.wait()


def call(body, ins, outs, scratch=(), flops=0, hbm_in=(), hbm_out=(), aliases=None):
    def spec(n, hbm):
        return pl.BlockSpec(memory_space=pltpu.HBM if n in hbm else pltpu.VMEM)

    moved = sum(a.size * a.dtype.itemsize for a in ins)
    moved += sum(int(np.prod(s)) * jnp.dtype(d).itemsize for s, d in outs)
    return pl.pallas_call(
        body,
        in_specs=[spec(n, hbm_in) for n in range(len(ins))],
        out_specs=[spec(n, hbm_out) for n in range(len(outs))],
        out_shape=[jax.ShapeDtypeStruct(s, d) for s, d in outs],
        scratch_shapes=list(scratch),
        input_output_aliases=aliases or {},
        compiler_params=pltpu.CompilerParams(vmem_limit_bytes=VMEM_LIMIT),
        cost_estimate=pl.CostEstimate(flops=flops, bytes_accessed=moved, transcendentals=0),
    )(*ins)


def move(value, axis, step):
    count = lax.axis_size(axis)
    return lax.ppermute(value, axis, [(i, (i + step) % count) for i in range(count)])


def local(flow_field):
    comps, ny, nz, nx = flow_field.shape
    assert ny == ROWS and nz == ROWS and nx % 1024 == 0
    assert lax.axis_size("gy") >= 5 and lax.axis_size("gz") >= 5
    half, quarter, lanes = nx // 2, nx // 4, nx // 128
    pairs = {k: [jnp.asarray(p) for p in v] for k, v in tables(nx).items()}
    field = pltpu.with_memory_space_constraint(flow_field, pltpu.HBM)
    flat = pltpu.with_memory_space_constraint(flow_field.reshape(comps, ROWS * ROWS, nx), pltpu.HBM)

    def consts(*names):
        return [p for n in names for p in pairs[n]]

    def dma(*shape):
        return pltpu.SemaphoreType.DMA(shape)

    edge = ((comps, 2, ROWS, nx), F32)
    y_right, y_left = call(
        edge_kernel,
        [field],
        [edge] * 2,
        [pltpu.VMEM((comps, 7, ROWS, nx), F32), dma(comps, 2)],
        hbm_in=(0,),
    )
    from_left0 = move(y_right, "gy", 1)
    from_right0 = move(y_left, "gy", -1)

    near = ((comps, 64, half), F32)
    far = ((comps, 16, half), F32)
    cells = ((comps, lanes, ROWS * ROWS, 128), F32)
    u, high, low, z_right, z_left, z_right2, z_left2 = call(
        lift_kernel,
        [flat] + consts("tx", "rims", "zsend", "tx12"),
        [cells] + [((comps, ROWS * ROWS, half), BF16)] * 2 + [near] * 2 + [far] * 2,
        [pltpu.VMEM((comps, ROWS * ROWS, nx), F32), pltpu.VMEM((comps, 128, half), F32), dma(comps)],
        flops=1 << 33,
        hbm_in=(0,),
    )
    z_from_left2 = move(z_right2, "gz", 2)
    z_from_left = move(z_right, "gz", 1)
    z_from_right = move(z_left, "gz", -1)
    z_from_right2 = move(z_left2, "gz", -2)

    first, second, token = call(
        own_kernel,
        [high, low] + consts("zown", "tx12", "ychain1", "ychain2"),
        [((comps, 112, half), F32), ((comps, 64, quarter), F32)] + [((8, 128), F32)],
        [pltpu.VMEM((comps, 64, half), F32)],
        flops=1 << 32,
    )

    planes = ((comps, lanes, 2, ROWS, 128), F32)
    b, z0_right, z0_left = call(
        along_y_kernel,
        [token, z_from_left2, z_from_right2, u, from_left0, from_right0] + consts("tx", "rims"),
        [cells] + [planes] * 2,
        [pltpu.VMEM((lanes, 64 * comps, 128), F32)],
        flops=1 << 32,
    )
    z0_from_left = move(z0_right, "gz", 1)
    z0_from_right = move(z0_left, "gz", -1)

    o1, o2, y1_right, y1_left, y2_right, y2_left = call(
        chain_kernel,
        [first, second, z_from_left, z_from_right, z_from_left2, z_from_right2] + consts("chain1", "chain2", "tx12"),
        [((comps, 64, half), F32), ((comps, 16, quarter), F32)]
        + [((comps, 32, half), F32)] * 2
        + [((comps, 8, quarter), F32)] * 2,
        [pltpu.VMEM((comps, 64, half), F32)],
        flops=1 << 31,
    )
    y_from_left2 = move(y2_right, "gy", 2)
    y_from_left = move(y1_right, "gy", 1)
    y_from_right = move(y1_left, "gy", -1)
    y_from_right2 = move(y2_left, "gy", -2)

    whole = ((comps, ROWS * ROWS, nx), F32)
    result, even = call(
        along_z_kernel,
        [b, z0_from_left, z0_from_right],
        [whole, ((comps, lanes // 2, ROWS * ROWS // 2, 128), F32)],
        [pltpu.VMEM((comps, lanes, ROWS * ROWS, 128), F32), dma(comps)],
        flops=1 << 32,
        hbm_out=(0,),
    )
    (result,) = call(
        last_kernel,
        [result, even, o1, o2, y_from_left, y_from_right, y_from_left2, y_from_right2]
        + consts("ygive1", "ygive2", "tx1"),
        [whole],
        [pltpu.VMEM((comps, lanes // 2, ROWS * ROWS // 2, 128), F32), dma(comps)],
        flops=1 << 30,
        hbm_in=(0,),
        hbm_out=(0,),
        aliases={0: 0},
    )
    return result.reshape(flow_field.shape)


def solution(mesh):
    placed = P(None, "gy", "gz", None)
    return jax.shard_map(local, mesh=mesh, in_specs=(placed,), out_specs=placed, check_vma=False)
```

```python
import jax
import jax.numpy as jnp
import ml_dtypes
import numpy as np
from jax import lax
from jax.experimental import pallas as pl
from jax.experimental.pallas import tpu as pltpu
from jax.sharding import PartitionSpec as P

ALPHA = -1.586134342059924
BETA = -0.052980118572961
GAMMA = 0.882911075530934
DELTA = 0.443506852043971
KAPPA = 1.149604398860241

F32 = jnp.float32
BF16 = jnp.bfloat16
VMEM_LIMIT = 32 * 1024 * 1024
ROWS = 16


def pair_matrix(length):
    cells = np.eye(length)
    even, odd = cells[0::2].copy(), cells[1::2].copy()
    odd = odd + ALPHA * (even + np.roll(even, -1, 0))
    even = even + BETA * (odd + np.roll(odd, 1, 0))
    odd = odd + GAMMA * (even + np.roll(even, -1, 0))
    even = even + DELTA * (odd + np.roll(odd, 1, 0))
    return even * KAPPA, odd / KAPPA


def alternated(length):
    low, high = pair_matrix(length)
    table = np.zeros((length, length))
    table[0::2], table[1::2] = low, high
    return table


def chain_blocks():
    count = 8
    length = count * ROWS
    first = alternated(length)
    second = alternated(length // 2) @ first[0::2]
    third = alternated(length // 4) @ second[0::2]
    result = []
    for table, per in ((first, 16), (second, 8), (third, 4)):
        here = table[4 * per : 5 * per]
        result.append({k: here[:, (4 + k) * ROWS : (5 + k) * ROWS] for k in (-2, -1, 0, 1, 2)})
    return result


def factor(block, rank):
    left, size, right = np.linalg.svd(block, full_matrices=False)
    assert np.all(size[rank:] < 1e-12)
    return left[:, :rank] * size[:rank], right[:rank]


def split_const(table):
    table = np.asarray(table, np.float64)
    high = table.astype(ml_dtypes.bfloat16)
    low = (table - high.astype(np.float64)).astype(ml_dtypes.bfloat16)
    return high, low


def stack(*parts):
    return np.concatenate(parts, 0)


def tables(nx):
    first, second, third = chain_blocks()
    eye = np.eye
    sides = (-1, 1)
    out = {}
    give1, send1, give2a, give2b, send2 = {}, {}, {}, {}, {}
    give2, send2d, give22, send22 = {}, {}, {}, {}
    for s in sides:
        give1[s], send1[s] = factor(second[s], 3)
        give2a[s] = third[s] @ send1[s].T
        give2b[s], send2[s] = factor(third[s] - give2a[s] @ send1[s], 2)
        give2[s], send2d[s] = factor(third[s], 4)
        give22[s], send22[s] = factor(third[2 * s], 2)

    low, high = pair_matrix(nx)
    out["tx"] = np.concatenate([low[128:256, 256:512], high[128:256, 256:512]], 0).T
    blocks = nx // 256
    rims = np.zeros((8 * blocks, nx))
    for j in range(blocks):
        block = np.concatenate([low[128 * j : 128 * j + 128], high[128 * j : 128 * j + 128]], 0).T
        after = (j + 1) % blocks
        rims[8 * j : 8 * j + 4, 256 * j : 256 * j + 256] = block[(256 * j - np.arange(4, 0, -1)) % nx]
        rims[8 * after + 4 : 8 * after + 8, 256 * j : 256 * j + 256] = block[256 * after : 256 * after + 4]
    low, high = pair_matrix(nx // 2)
    tx1 = np.concatenate([low, high], 0).T
    low, high = pair_matrix(nx // 4)
    tx2 = np.concatenate([low, high], 0).T
    out["tx1"] = tx1
    out["tx12"] = tx1[:, : nx // 4] @ tx2

    def planes(send):
        return np.einsum("pz,ab->paBz".replace("B", "b"), send, eye(ROWS)).reshape(-1, ROWS * ROWS)

    out["zsend"] = stack(*[planes(send[s]) for send in (send1, send2, send22) for s in sides])
    out["zown"] = stack(np.kron(eye(ROWS), second[0]), np.kron(eye(ROWS), third[0]))

    def back(give):
        return np.einsum("zp,ab->azpb", give, eye(ROWS)).reshape(ROWS * give.shape[0], -1)

    zgive1 = np.concatenate([back(give1[s]) for s in sides], 1)
    zgive2a = np.concatenate([back(give2a[s]) for s in sides], 1)
    zgive2b = np.concatenate([back(give2b[s]) for s in sides] + [back(give22[s]) for s in sides], 1)
    out["ychain1"] = stack(np.kron(second[0], eye(8)), *[np.kron(send1[s], eye(8)) for s in sides])
    out["ychain2"] = stack(
        np.kron(third[0], eye(4)),
        *[np.kron(send2d[s], eye(4)) for s in sides],
        *[np.kron(send22[s], eye(4)) for s in sides],
    )
    out["chain1"] = stack(out["ychain1"] @ zgive1, out["ychain2"] @ zgive2a)
    out["chain2"] = out["ychain2"] @ zgive2b
    out["ygive1"] = np.concatenate([np.kron(give1[s], eye(8)) for s in sides], 1)
    out["ygive2"] = np.concatenate(
        [np.kron(give2[s], eye(4)) for s in sides] + [np.kron(give22[s], eye(4)) for s in sides], 1
    )
    pairs = {name: split_const(table) for name, table in out.items()}
    high, low = split_const(rims)
    pairs["rims"] = (np.concatenate([high, high, low, np.zeros_like(high)], 0),)
    return pairs


def split(value):
    high = value.astype(BF16)
    low = (value - high.astype(F32)).astype(BF16)
    return high, low


def dot(a, b):
    return jnp.dot(a, b, preferred_element_type=F32)


def left(table, rows):
    return dot(table[0], rows[0]) + (dot(table[0], rows[1]) + dot(table[1], rows[0]))


def right(rows, table):
    return dot(rows[0], table[0]) + (dot(rows[0], table[1]) + dot(rows[1], table[0]))


def both(high_ref, low_ref):
    return high_ref[...], low_ref[...]


def lift_line(cells, before, after):
    even, odd = list(cells[0::2]), list(cells[1::2])
    count = len(even)
    even.append(after[0])
    odd = [odd[n] + ALPHA * (even[n] + even[n + 1]) for n in range(count)]
    odd_before = before[0] + ALPHA * even[0]
    even_before = before[1] + BETA * odd_before
    odd_around = [odd_before] + odd + [after[1]]
    even = [even[n] + BETA * (odd_around[n + 1] + odd_around[n]) for n in range(count + 1)]
    odd = [odd[n] + GAMMA * (even[n] + even[n + 1]) for n in range(count)]
    odd_around = [odd_before + GAMMA * (even_before + even[0])] + odd
    even = [even[n] + DELTA * (odd_around[n + 1] + odd_around[n]) for n in range(count)]
    result = []
    for n in range(count):
        result += [even[n] * KAPPA, odd[n] * (1.0 / KAPPA)]
    return result


def give_right(cells):
    a, b, c, d = cells
    return d + ALPHA * c, c + BETA * (b + ALPHA * (a + c))


def give_left(cells):
    a, b, c = cells
    return a, b + ALPHA * (a + c)


def lift_x(cells, table, rims_ref, store):
    count, nx = cells.shape
    lane = lax.broadcasted_iota(jnp.int32, (count, 128), 1)
    rims = None
    for j in range(nx // 256):
        at = 256 * j
        before = cells[:, nx - 128 :] if j == 0 else cells[:, at - 128 : at]
        rim = jnp.where(lane >= 124, before, jnp.where(lane < 4, cells[:, at : at + 128], 0.0))
        rim = pltpu.roll(rim, 4 + 8 * j, 1)
        rims = rim if rims is None else rims + rim
    width = nx // 32
    high = rims.astype(BF16).astype(F32)
    rims = (high + pltpu.roll(rims - high, width, 1) + pltpu.roll(high, 2 * width, 1)).astype(BF16)
    parts = split(cells)
    for j in range(nx // 256):
        lanes = slice(256 * j, 256 * j + 256)
        store(j, right([part[:, lanes] for part in parts], table) + dot(rims, rims_ref[:, lanes]))


def edge_kernel(x_ref, to_right_ref, to_left_ref, rows_ref, sems):
    comps = x_ref.shape[0]
    copies = []
    for c in range(comps):
        copies.append(pltpu.make_async_copy(x_ref.at[c, pl.ds(0, 3)], rows_ref.at[c, pl.ds(0, 3)], sems.at[c, 0]))
        copies.append(pltpu.make_async_copy(x_ref.at[c, pl.ds(12, 4)], rows_ref.at[c, pl.ds(3, 4)], sems.at[c, 1]))
    for copy in copies:
        copy.start()
    for c in range(comps):
        copies[2 * c].wait()
        to_left_ref[c, 0], to_left_ref[c, 1] = give_left([rows_ref[c, k] for k in range(3)])
        copies[2 * c + 1].wait()
        to_right_ref[c, 0], to_right_ref[c, 1] = give_right([rows_ref[c, k] for k in range(3, 7)])


def lift_kernel(
    x_ref, txh, txl, rims, zsh, zsl, t12h, t12l,
    u_ref, high_ref, low_ref, r1_ref, l1_ref, r2_ref, l2_ref, cells_ref, far_ref, sems,
):
    comps, _, nx = x_ref.shape
    blocks, quarter = nx // 256, nx // 4

    def copy(c):
        return pltpu.make_async_copy(x_ref.at[c], cells_ref.at[c], sems.at[c])

    copy(0).start()
    copy(1).start()

    def step(c, _):
        copy(c).wait()

        @pl.when(c + 2 < comps)
        def _():
            copy(c + 2).start()

        def store(j, value):
            u_ref[c, j] = value[:, :128]
            u_ref[c, blocks + j] = value[:, 128:]
            high, low = split(value[:, :128])
            high_ref[c, :, 128 * j : 128 * j + 128] = high
            low_ref[c, :, 128 * j : 128 * j + 128] = low

        lift_x(cells_ref[c], both(txh, txl), rims, store)
        rows = left(both(zsh, zsl), (high_ref[c], low_ref[c]))
        r1_ref[c, :48] = rows[:48]
        l1_ref[c, :48] = rows[48:96]
        far_ref[c] = rows[96:]
        return 0

    lax.fori_loop(0, comps, step, 0)
    far = right(split(far_ref[...].reshape(128 * comps, nx // 2)), both(t12h, t12l))
    for c in range(comps):
        for k, (ref, ref2) in enumerate(((r1_ref, r2_ref), (l1_ref, l2_ref))):
            for p in range(2):
                lanes = slice(quarter * p, quarter * p + quarter)
                at = 128 * c + 32 * k + 16 * p
                ref[c, 48:, lanes] = far[at : at + 16]
                ref2[c, :, lanes] = far[at + 64 : at + 80]


def own_kernel(
    high_ref, low_ref, zoh, zol, t12h, t12l, c1h, c1l, c2h, c2l, first_ref, second_ref, token_ref, far_ref,
):
    comps, _, half = high_ref.shape
    token_ref[...] = jnp.zeros_like(token_ref)

    def step(c, _):
        rows = left(both(zoh, zol), (high_ref[c], low_ref[c]))
        first_ref[c] = left(both(c1h, c1l), split(rows[:128]))
        far_ref[c] = rows[128:]
        return 0

    lax.fori_loop(0, comps, step, 0)
    far = right(split(far_ref[...].reshape(64 * comps, half)), both(t12h, t12l))
    for c in range(comps):
        second_ref[c] = left(both(c2h, c2l), split(far[64 * c : 64 * c + 64]))


def chain_kernel(
    first_ref, second_ref, l1_ref, r1_ref, l2_ref, r2_ref,
    g1h, g1l, g2h, g2l, t12h, t12l,
    o1_ref, o2_ref, to_r_ref, to_l_ref, away_ref, far_ref,
):
    comps, _, half = first_ref.shape
    quarter = half // 2

    def step(c, _):
        near = split(jnp.concatenate([l1_ref[c, :48], r1_ref[c, :48]], 0))
        rows = left(both(g1h, g1l), near)
        far_ref[c] = rows[112:]
        first = first_ref[c] + rows[:112]
        o1_ref[c] = first[:64]
        to_r_ref[c, :24] = first[64:88]
        to_l_ref[c, :24] = first[88:]
        return 0

    lax.fori_loop(0, comps, step, 0)
    far = right(split(far_ref[...].reshape(64 * comps, half)), both(t12h, t12l))
    for c in range(comps):
        deep = []
        for ref in (l1_ref, r1_ref):
            deep += [ref[c, 48:, :quarter], ref[c, 48:, quarter:]]
        for ref in (l2_ref, r2_ref):
            deep += [ref[c, :, :quarter], ref[c, :, quarter:]]
        second = left(both(g2h, g2l), split(jnp.concatenate(deep, 0)))
        second = second_ref[c] + (far[64 * c : 64 * c + 64] + second)
        o2_ref[c] = second[:16]
        for k, ref in enumerate((to_r_ref, to_l_ref)):
            ref[c, 24:, :quarter] = second[16 + 16 * k : 24 + 16 * k]
            ref[c, 24:, quarter:] = second[24 + 16 * k : 32 + 16 * k]
        away_ref[c] = second[48:]


def along_y_kernel(_, u_ref, l_ref, r_ref, txh, txl, rims, b_ref, to_r_ref, to_l_ref, halo_ref):
    comps, lanes = u_ref.shape[:2]
    blocks = lanes // 2

    def store(j, value):
        halo_ref[j] = value[:, :128]
        halo_ref[blocks + j] = value[:, 128:]

    rows = [ref[c, p] for c in range(comps) for ref in (l_ref, r_ref) for p in range(2)]
    lift_x(jnp.concatenate(rows, 0), both(txh, txl), rims, store)

    def step(n, _):
        c, k = n // lanes, n % lanes
        u, b, halo = u_ref.at[c, k], b_ref.at[c, k], halo_ref.at[k]
        for part in range(2):
            cells = [u[16 * y + 8 * part : 16 * y + 8 * part + 8] for y in range(ROWS)]
            around = [halo[pl.ds(pl.multiple_of(64 * c + 16 * p + 8 * part, 8), 8)] for p in range(4)]
            for y, value in enumerate(lift_line(cells, around[:2], around[2:])):
                b[pl.ds(128 * part + y, 8, stride=ROWS)] = value

        def plane(z):
            return b[16 * z : 16 * z + 16]

        to_r_ref[c, k, 0], to_r_ref[c, k, 1] = give_right([plane(z) for z in range(12, 16)])
        to_l_ref[c, k, 0], to_l_ref[c, k, 1] = give_left([plane(z) for z in range(3)])
        return 0

    lax.fori_loop(0, comps * lanes, step, 0)


def after(values, earlier):
    count = len(values)

    def body(*refs):
        pass

    return pl.pallas_call(
        body,
        in_specs=[pl.BlockSpec(memory_space=pl.ANY)] * (count + len(earlier)),
        out_specs=[pl.BlockSpec(memory_space=pl.ANY)] * count,
        out_shape=[jax.ShapeDtypeStruct(v.shape, v.dtype) for v in values],
        input_output_aliases={n: n for n in range(count)},
    )(*values, *earlier)


def away_kernel(_, away_ref, to_r2_ref, to_l2_ref):
    to_r2_ref[...] = away_ref[:, :8]
    to_l2_ref[...] = away_ref[:, 8:]


def along_z_kernel(b_ref, l_ref, r_ref, out_ref, even_ref, done_ref, sems):
    comps, lanes = b_ref.shape[:2]

    def copy(c, k):
        return pltpu.make_async_copy(
            done_ref.at[c, k], out_ref.at[c, :, pl.ds(pl.multiple_of(128 * k, 128), 128)], sems.at[c]
        )

    def step(n, _):
        c, k = n // lanes, n % lanes
        b, done = b_ref.at[c, k], done_ref.at[c, k]
        for part in range(2):
            cells = [b[16 * z + 8 * part : 16 * z + 8 * part + 8] for z in range(ROWS)]
            around = [ref[c, k, p, 8 * part : 8 * part + 8] for ref in (l_ref, r_ref) for p in range(2)]
            for z, value in enumerate(lift_line(cells, around[:2], around[2:])):
                done[pl.ds(128 * part + z, 8, stride=ROWS)] = value
        copy(c, k).start()

        @pl.when(k < lanes // 2)
        def _():
            for y in range(ROWS // 2):
                even_ref[c, k, 16 * y : 16 * y + 16] = done[32 * y : 32 * y + 16]

        return 0

    lax.fori_loop(0, comps * lanes, step, 0)
    for c in range(comps):
        for k in range(lanes):
            copy(c, k).wait()


def last_kernel(
    _, even_ref, o1_ref, o2_ref, l1_ref, r1_ref, l2_ref, r2_ref,
    g1h, g1l, g2h, g2l, t1h, t1l, out_ref, done_ref, sems,
):
    comps, lanes = even_ref.shape[:2]
    half = 128 * lanes
    quarter = half // 2
    window, deepest = [], []
    for c in range(comps):
        near = split(jnp.concatenate([l1_ref[c, :24], r1_ref[c, :24]], 0))
        window.append(o1_ref[c] + left(both(g1h, g1l), near))
        deep = []
        for ref in (l1_ref, r1_ref):
            deep += [ref[c, 24:, :quarter], ref[c, 24:, quarter:]]
        deep += [l2_ref[c], r2_ref[c]]
        deepest.append(o2_ref[c] + left(both(g2h, g2l), split(jnp.concatenate(deep, 0))))
    window = right(split(jnp.concatenate(window, 0)), both(t1h, t1l))
    copies = []
    for c in range(comps):
        for k in range(lanes):
            at = slice(128 * k, 128 * k + 128)
            done = done_ref.at[c, k]
            done[...] = even_ref[c, k]
            for y in range(8):
                done[pl.ds(16 * y, 8, stride=2)] = window[64 * c + 8 * y : 64 * c + 8 * y + 8, at]
            if 128 * k < quarter:
                for y in range(4):
                    done[pl.ds(32 * y, 4, stride=4)] = deepest[c][4 * y : 4 * y + 4, at]
            for y in range(8):
                copies.append(
                    pltpu.make_async_copy(done.at[pl.ds(16 * y, 16)], out_ref.at[c, pl.ds(32 * y, 16), at], sems.at[c])
                )
                copies[-1].start()
    for copy in copies:
        copy.wait()


def call(body, ins, outs, scratch=(), flops=0, hbm_in=(), hbm_out=(), aliases=None):
    def spec(n, hbm):
        return pl.BlockSpec(memory_space=pltpu.HBM if n in hbm else pltpu.VMEM)

    moved = sum(a.size * a.dtype.itemsize for a in ins)
    moved += sum(int(np.prod(s)) * jnp.dtype(d).itemsize for s, d in outs)
    return pl.pallas_call(
        body,
        in_specs=[spec(n, hbm_in) for n in range(len(ins))],
        out_specs=[spec(n, hbm_out) for n in range(len(outs))],
        out_shape=[jax.ShapeDtypeStruct(s, d) for s, d in outs],
        scratch_shapes=list(scratch),
        input_output_aliases=aliases or {},
        compiler_params=pltpu.CompilerParams(vmem_limit_bytes=VMEM_LIMIT),
        cost_estimate=pl.CostEstimate(flops=flops, bytes_accessed=moved, transcendentals=0),
    )(*ins)


def move(value, axis, step):
    count = lax.axis_size(axis)
    return lax.ppermute(value, axis, [(i, (i + step) % count) for i in range(count)])


def local(flow_field):
    comps, ny, nz, nx = flow_field.shape
    assert ny == ROWS and nz == ROWS and nx % 1024 == 0
    assert lax.axis_size("gy") >= 5 and lax.axis_size("gz") >= 5
    half, quarter, lanes = nx // 2, nx // 4, nx // 128
    pairs = {k: [jnp.asarray(p) for p in v] for k, v in tables(nx).items()}
    field = pltpu.with_memory_space_constraint(flow_field, pltpu.HBM)
    flat = pltpu.with_memory_space_constraint(flow_field.reshape(comps, ROWS * ROWS, nx), pltpu.HBM)

    def consts(*names):
        return [p for n in names for p in pairs[n]]

    def dma(*shape):
        return pltpu.SemaphoreType.DMA(shape)

    edge = ((comps, 2, ROWS, nx), F32)
    y_right, y_left = call(
        edge_kernel,
        [field],
        [edge] * 2,
        [pltpu.VMEM((comps, 7, ROWS, nx), F32), dma(comps, 2)],
        hbm_in=(0,),
    )
    from_left0 = move(y_right, "gy", 1)
    from_right0 = move(y_left, "gy", -1)

    near = ((comps, 64, half), F32)
    far = ((comps, 16, half), F32)
    cells = ((comps, lanes, ROWS * ROWS, 128), F32)
    u, high, low, z_right, z_left, z_right2, z_left2 = call(
        lift_kernel,
        [flat] + consts("tx", "rims", "zsend", "tx12"),
        [cells] + [((comps, ROWS * ROWS, half), BF16)] * 2 + [near] * 2 + [far] * 2,
        [pltpu.VMEM((comps, ROWS * ROWS, nx), F32), pltpu.VMEM((comps, 128, half), F32), dma(comps)],
        flops=1 << 33,
        hbm_in=(0,),
    )
    z_from_left = move(z_right, "gz", 1)
    z_from_right = move(z_left, "gz", -1)
    z_from_left2 = move(z_right2, "gz", 2)

    first, second, token = call(
        own_kernel,
        [high, low] + consts("zown", "tx12", "ychain1", "ychain2"),
        [((comps, 112, half), F32), ((comps, 64, quarter), F32)] + [((8, 128), F32)],
        [pltpu.VMEM((comps, 64, half), F32)],
        flops=1 << 32,
    )

    (z_left2,) = after([z_left2], [token, z_from_left2])
    z_from_right2 = move(z_left2, "gz", -2)

    planes = ((comps, lanes, 2, ROWS, 128), F32)
    b, z0_right, z0_left = call(
        along_y_kernel,
        [token, u, from_left0, from_right0] + consts("tx", "rims"),
        [cells] + [planes] * 2,
        [pltpu.VMEM((lanes, 64 * comps, 128), F32)],
        flops=1 << 32,
    )
    z0_right, z0_left = after([z0_right, z0_left], [z_from_right2])
    z0_from_left = move(z0_right, "gz", 1)
    z0_from_right = move(z0_left, "gz", -1)

    o1, o2, y1_right, y1_left, away = call(
        chain_kernel,
        [first, second, z_from_left, z_from_right, z_from_left2, z_from_right2] + consts("chain1", "chain2", "tx12"),
        [((comps, 64, half), F32), ((comps, 16, quarter), F32)]
        + [((comps, 32, half), F32)] * 2
        + [((comps, 16, quarter), F32)],
        [pltpu.VMEM((comps, 64, half), F32)],
        flops=1 << 31,
    )
    y_from_left = move(y1_right, "gy", 1)
    y_from_right = move(y1_left, "gy", -1)
    y2_right, y2_left = call(away_kernel, [z0_from_left, away], [((comps, 8, quarter), F32)] * 2)
    y_from_left2 = move(y2_right, "gy", 2)
    y_from_right2 = move(y2_left, "gy", -2)

    whole = ((comps, ROWS * ROWS, nx), F32)
    result, even = call(
        along_z_kernel,
        [b, z0_from_left, z0_from_right],
        [whole, ((comps, lanes // 2, ROWS * ROWS // 2, 128), F32)],
        [pltpu.VMEM((comps, lanes, ROWS * ROWS, 128), F32), dma(comps)],
        flops=1 << 32,
        hbm_out=(0,),
    )
    (result,) = call(
        last_kernel,
        [result, even, o1, o2, y_from_left, y_from_right, y_from_left2, y_from_right2]
        + consts("ygive1", "ygive2", "tx1"),
        [whole],
        [pltpu.VMEM((comps, lanes // 2, ROWS * ROWS // 2, 128), F32), dma(comps)],
        flops=1 << 30,
        hbm_in=(0,),
        hbm_out=(0,),
        aliases={0: 0},
    )
    return result.reshape(flow_field.shape)


def solution(mesh):
    placed = P(None, "gy", "gz", None)
    return jax.shard_map(local, mesh=mesh, in_specs=(placed,), out_specs=placed, check_vma=False)
```

```python
import jax
import jax.numpy as jnp
import ml_dtypes
import numpy as np
from jax import lax
from jax.experimental import pallas as pl
from jax.experimental.pallas import tpu as pltpu
from jax.sharding import PartitionSpec as P

ALPHA = -1.586134342059924
BETA = -0.052980118572961
GAMMA = 0.882911075530934
DELTA = 0.443506852043971
KAPPA = 1.149604398860241

F32 = jnp.float32
BF16 = jnp.bfloat16
VMEM_LIMIT = 32 * 1024 * 1024
ROWS = 16


def pair_matrix(length):
    cells = np.eye(length)
    even, odd = cells[0::2].copy(), cells[1::2].copy()
    odd = odd + ALPHA * (even + np.roll(even, -1, 0))
    even = even + BETA * (odd + np.roll(odd, 1, 0))
    odd = odd + GAMMA * (even + np.roll(even, -1, 0))
    even = even + DELTA * (odd + np.roll(odd, 1, 0))
    return even * KAPPA, odd / KAPPA


def alternated(length):
    low, high = pair_matrix(length)
    table = np.zeros((length, length))
    table[0::2], table[1::2] = low, high
    return table


def chain_blocks():
    count = 8
    length = count * ROWS
    first = alternated(length)
    second = alternated(length // 2) @ first[0::2]
    third = alternated(length // 4) @ second[0::2]
    result = []
    for table, per in ((first, 16), (second, 8), (third, 4)):
        here = table[4 * per : 5 * per]
        result.append({k: here[:, (4 + k) * ROWS : (5 + k) * ROWS] for k in (-2, -1, 0, 1, 2)})
    return result


def factor(block, rank):
    left, size, right = np.linalg.svd(block, full_matrices=False)
    assert np.all(size[rank:] < 1e-12)
    return left[:, :rank] * size[:rank], right[:rank]


def split_const(table):
    table = np.asarray(table, np.float64)
    high = table.astype(ml_dtypes.bfloat16)
    low = (table - high.astype(np.float64)).astype(ml_dtypes.bfloat16)
    return high, low


def stack(*parts):
    return np.concatenate(parts, 0)


def tables(nx):
    first, second, third = chain_blocks()
    eye = np.eye
    sides = (-1, 1)
    out = {}
    give1, send1, give2a, give2b, send2 = {}, {}, {}, {}, {}
    give2, send2d, give22, send22 = {}, {}, {}, {}
    for s in sides:
        give1[s], send1[s] = factor(second[s], 3)
        give2a[s] = third[s] @ send1[s].T
        give2b[s], send2[s] = factor(third[s] - give2a[s] @ send1[s], 2)
        give2[s], send2d[s] = factor(third[s], 4)
        give22[s], send22[s] = factor(third[2 * s], 2)

    low, high = pair_matrix(nx)
    out["tx"] = np.concatenate([low[128:256, 256:512], high[128:256, 256:512]], 0).T
    blocks = nx // 256
    rims = np.zeros((8 * blocks, nx))
    for j in range(blocks):
        block = np.concatenate([low[128 * j : 128 * j + 128], high[128 * j : 128 * j + 128]], 0).T
        after = (j + 1) % blocks
        rims[8 * j : 8 * j + 4, 256 * j : 256 * j + 256] = block[(256 * j - np.arange(4, 0, -1)) % nx]
        rims[8 * after + 4 : 8 * after + 8, 256 * j : 256 * j + 256] = block[256 * after : 256 * after + 4]
    low, high = pair_matrix(nx // 2)
    tx1 = np.concatenate([low, high], 0).T
    low, high = pair_matrix(nx // 4)
    tx2 = np.concatenate([low, high], 0).T
    out["tx1"] = tx1
    out["tx12"] = tx1[:, : nx // 4] @ tx2

    def planes(send):
        return np.einsum("pz,ab->paBz".replace("B", "b"), send, eye(ROWS)).reshape(-1, ROWS * ROWS)

    zsend = [planes(send[s]) for send in (send1, send2, send22) for s in sides]

    def back(give):
        return np.einsum("zp,ab->azpb", give, eye(ROWS)).reshape(ROWS * give.shape[0], -1)

    zgive1 = np.concatenate([back(give1[s]) for s in sides], 1)
    zgive2a = np.concatenate([back(give2a[s]) for s in sides], 1)
    zgive2b = np.concatenate([back(give2b[s]) for s in sides] + [back(give22[s]) for s in sides], 1)
    ychain1 = stack(np.kron(second[0], eye(8)), *[np.kron(send1[s], eye(8)) for s in sides])
    ychain2 = stack(
        np.kron(third[0], eye(4)),
        *[np.kron(send2d[s], eye(4)) for s in sides],
        *[np.kron(send22[s], eye(4)) for s in sides],
    )
    own1, own2 = np.kron(eye(ROWS), second[0]), np.kron(eye(ROWS), third[0])
    out["zsend"] = stack(*zsend, ychain2 @ own2, ychain1 @ own1)
    out["chain1"] = stack(ychain1 @ zgive1, ychain2 @ zgive2a)
    out["chain2"] = ychain2 @ zgive2b
    out["ygive1"] = np.concatenate([np.kron(give1[s], eye(8)) for s in sides], 1)
    out["ygive2"] = np.concatenate(
        [np.kron(give2[s], eye(4)) for s in sides] + [np.kron(give22[s], eye(4)) for s in sides], 1
    )
    pairs = {name: split_const(table) for name, table in out.items()}
    high, low = split_const(rims)
    pairs["rims"] = (np.concatenate([high, high, low, np.zeros_like(high)], 0),)
    return pairs


def split(value):
    high = value.astype(BF16)
    low = (value - high.astype(F32)).astype(BF16)
    return high, low


def dot(a, b):
    return jnp.dot(a, b, preferred_element_type=F32)


def left(table, rows):
    return dot(table[0], rows[0]) + (dot(table[0], rows[1]) + dot(table[1], rows[0]))


def right(rows, table):
    return dot(rows[0], table[0]) + (dot(rows[0], table[1]) + dot(rows[1], table[0]))


def both(high_ref, low_ref):
    return high_ref[...], low_ref[...]


def lift_line(cells, before, after):
    even, odd = list(cells[0::2]), list(cells[1::2])
    count = len(even)
    even.append(after[0])
    odd = [odd[n] + ALPHA * (even[n] + even[n + 1]) for n in range(count)]
    odd_before = before[0] + ALPHA * even[0]
    even_before = before[1] + BETA * odd_before
    odd_around = [odd_before] + odd + [after[1]]
    even = [even[n] + BETA * (odd_around[n + 1] + odd_around[n]) for n in range(count + 1)]
    odd = [odd[n] + GAMMA * (even[n] + even[n + 1]) for n in range(count)]
    odd_around = [odd_before + GAMMA * (even_before + even[0])] + odd
    even = [even[n] + DELTA * (odd_around[n + 1] + odd_around[n]) for n in range(count)]
    result = []
    for n in range(count):
        result += [even[n] * KAPPA, odd[n] * (1.0 / KAPPA)]
    return result


def give_right(cells):
    a, b, c, d = cells
    return d + ALPHA * c, c + BETA * (b + ALPHA * (a + c))


def give_left(cells):
    a, b, c = cells
    return a, b + ALPHA * (a + c)


def lift_x(cells, table, rims_ref, store):
    count, nx = cells.shape
    lane = lax.broadcasted_iota(jnp.int32, (count, 128), 1)
    rims = None
    for j in range(nx // 256):
        at = 256 * j
        before = cells[:, nx - 128 :] if j == 0 else cells[:, at - 128 : at]
        rim = jnp.where(lane >= 124, before, jnp.where(lane < 4, cells[:, at : at + 128], 0.0))
        rim = pltpu.roll(rim, 4 + 8 * j, 1)
        rims = rim if rims is None else rims + rim
    width = nx // 32
    high = rims.astype(BF16).astype(F32)
    rims = (high + pltpu.roll(rims - high, width, 1) + pltpu.roll(high, 2 * width, 1)).astype(BF16)
    parts = split(cells)
    for j in range(nx // 256):
        lanes = slice(256 * j, 256 * j + 256)
        store(j, right([part[:, lanes] for part in parts], table) + dot(rims, rims_ref[:, lanes]))


def edge_kernel(x_ref, to_right_ref, to_left_ref, head_ref, rows_ref, sems, head_sem):
    comps = x_ref.shape[0]
    copies = []
    for c in range(comps):
        copies.append(pltpu.make_async_copy(x_ref.at[c, pl.ds(0, 3)], rows_ref.at[c, pl.ds(0, 3)], sems.at[c, 0]))
        copies.append(pltpu.make_async_copy(x_ref.at[c, pl.ds(12, 4)], rows_ref.at[c, pl.ds(3, 4)], sems.at[c, 1]))
    head = pltpu.make_async_copy(x_ref.at[0], head_ref, head_sem)
    for copy in copies:
        copy.start()
    head.start()
    for c in range(comps):
        copies[2 * c].wait()
        to_left_ref[c, 0], to_left_ref[c, 1] = give_left([rows_ref[c, k] for k in range(3)])
        copies[2 * c + 1].wait()
        to_right_ref[c, 0], to_right_ref[c, 1] = give_right([rows_ref[c, k] for k in range(3, 7)])
    head.wait()


def lift_kernel(
    x_ref, head_ref, txh, txl, rims, zsh, zsl, t12h, t12l,
    u_ref, first_ref, second_ref, r1_ref, l1_ref, r2_ref, l2_ref, cells_ref, high_ref, low_ref, far_ref, sems,
):
    comps, _, nx = x_ref.shape
    blocks, quarter = nx // 256, nx // 4

    def copy(c):
        return pltpu.make_async_copy(x_ref.at[c], cells_ref.at[c], sems.at[c])

    for c in range(1, comps):
        copy(c).start()

    def part(c, cells):
        def store(j, value):
            u_ref[c, j] = value[:, :128]
            u_ref[c, blocks + j] = value[:, 128:]
            high, low = split(value[:, :128])
            high_ref[:, 128 * j : 128 * j + 128] = high
            low_ref[:, 128 * j : 128 * j + 128] = low

        lift_x(cells, both(txh, txl), rims, store)
        rows = left(both(zsh, zsl), both(high_ref, low_ref))
        r1_ref[c, :48] = rows[:48]
        l1_ref[c, :48] = rows[48:96]
        far_ref[c] = rows[96:288]
        first_ref[c] = rows[288:]

    def step(c, _):
        copy(c).wait()
        part(c, cells_ref[c])
        return 0

    part(0, head_ref[...])
    lax.fori_loop(1, comps, step, 0)
    far = right(split(far_ref[...].reshape(192 * comps, nx // 2)), both(t12h, t12l))
    for c in range(comps):
        for k, (ref, ref2) in enumerate(((r1_ref, r2_ref), (l1_ref, l2_ref))):
            for p in range(2):
                lanes = slice(quarter * p, quarter * p + quarter)
                at = 192 * c + 32 * k + 16 * p
                ref[c, 48:, lanes] = far[at : at + 16]
                ref2[c, :, lanes] = far[at + 64 : at + 80]
        second_ref[c] = far[192 * c + 128 : 192 * c + 192]


def chain_kernel(
    first_ref, second_ref, l1_ref, r1_ref, l2_ref, r2_ref,
    g1h, g1l, g2h, g2l, t12h, t12l,
    o1_ref, o2_ref, to_r_ref, to_l_ref, away_ref, far_ref,
):
    comps, _, half = first_ref.shape
    quarter = half // 2

    def step(c, _):
        near = split(jnp.concatenate([l1_ref[c, :48], r1_ref[c, :48]], 0))
        rows = left(both(g1h, g1l), near)
        far_ref[c] = rows[112:]
        first = first_ref[c] + rows[:112]
        o1_ref[c] = first[:64]
        to_r_ref[c, :24] = first[64:88]
        to_l_ref[c, :24] = first[88:]
        return 0

    lax.fori_loop(0, comps, step, 0)
    far = right(split(far_ref[...].reshape(64 * comps, half)), both(t12h, t12l))
    for c in range(comps):
        deep = []
        for ref in (l1_ref, r1_ref):
            deep += [ref[c, 48:, :quarter], ref[c, 48:, quarter:]]
        for ref in (l2_ref, r2_ref):
            deep += [ref[c, :, :quarter], ref[c, :, quarter:]]
        second = left(both(g2h, g2l), split(jnp.concatenate(deep, 0)))
        second = second_ref[c] + (far[64 * c : 64 * c + 64] + second)
        o2_ref[c] = second[:16]
        for k, ref in enumerate((to_r_ref, to_l_ref)):
            ref[c, 24:, :quarter] = second[16 + 16 * k : 24 + 16 * k]
            ref[c, 24:, quarter:] = second[24 + 16 * k : 32 + 16 * k]
        away_ref[c] = second[48:]


def along_y_kernel(_, _2, u_ref, l_ref, r_ref, txh, txl, rims, b_ref, to_r_ref, to_l_ref, halo_ref):
    comps, lanes = u_ref.shape[:2]
    blocks = lanes // 2

    def store(j, value):
        halo_ref[j] = value[:, :128]
        halo_ref[blocks + j] = value[:, 128:]

    rows = [ref[c, p] for c in range(comps) for ref in (l_ref, r_ref) for p in range(2)]
    lift_x(jnp.concatenate(rows, 0), both(txh, txl), rims, store)

    def step(n, _):
        c, k = n // lanes, n % lanes
        u, b, halo = u_ref.at[c, k], b_ref.at[c, k], halo_ref.at[k]
        for part in range(2):
            cells = [u[16 * y + 8 * part : 16 * y + 8 * part + 8] for y in range(ROWS)]
            around = [halo[pl.ds(pl.multiple_of(64 * c + 16 * p + 8 * part, 8), 8)] for p in range(4)]
            for y, value in enumerate(lift_line(cells, around[:2], around[2:])):
                b[pl.ds(128 * part + y, 8, stride=ROWS)] = value

        def plane(z):
            return b[16 * z : 16 * z + 16]

        to_r_ref[c, k, 0], to_r_ref[c, k, 1] = give_right([plane(z) for z in range(12, 16)])
        to_l_ref[c, k, 0], to_l_ref[c, k, 1] = give_left([plane(z) for z in range(3)])
        return 0

    lax.fori_loop(0, comps * lanes, step, 0)


def away_kernel(_, away_ref, to_r2_ref, to_l2_ref):
    to_r2_ref[...] = away_ref[:, :8]
    to_l2_ref[...] = away_ref[:, 8:]


def along_z_kernel(b_ref, l_ref, r_ref, out_ref, even_ref, done_ref, sems):
    comps, lanes = b_ref.shape[:2]

    def copy(c, k):
        return pltpu.make_async_copy(
            done_ref.at[c, k], out_ref.at[c, :, pl.ds(pl.multiple_of(128 * k, 128), 128)], sems.at[c]
        )

    def step(n, _):
        c, k = n // lanes, n % lanes
        b, done = b_ref.at[c, k], done_ref.at[c, k]
        for part in range(2):
            cells = [b[16 * z + 8 * part : 16 * z + 8 * part + 8] for z in range(ROWS)]
            around = [ref[c, k, p, 8 * part : 8 * part + 8] for ref in (l_ref, r_ref) for p in range(2)]
            for z, value in enumerate(lift_line(cells, around[:2], around[2:])):
                done[pl.ds(128 * part + z, 8, stride=ROWS)] = value
        copy(c, k).start()

        @pl.when(k < lanes // 2)
        def _():
            for y in range(ROWS // 2):
                even_ref[c, k, 16 * y : 16 * y + 16] = done[32 * y : 32 * y + 16]

        return 0

    lax.fori_loop(0, comps * lanes, step, 0)
    for c in range(comps):
        for k in range(lanes):
            copy(c, k).wait()


def last_kernel(
    _, even_ref, o1_ref, o2_ref, l1_ref, r1_ref, l2_ref, r2_ref,
    g1h, g1l, g2h, g2l, t1h, t1l, out_ref, done_ref, sems,
):
    comps, lanes = even_ref.shape[:2]
    half = 128 * lanes
    quarter = half // 2
    window, deepest = [], []
    for c in range(comps):
        near = split(jnp.concatenate([l1_ref[c, :24], r1_ref[c, :24]], 0))
        window.append(o1_ref[c] + left(both(g1h, g1l), near))
        deep = []
        for ref in (l1_ref, r1_ref):
            deep += [ref[c, 24:, :quarter], ref[c, 24:, quarter:]]
        deep += [l2_ref[c], r2_ref[c]]
        deepest.append(o2_ref[c] + left(both(g2h, g2l), split(jnp.concatenate(deep, 0))))
    window = right(split(jnp.concatenate(window, 0)), both(t1h, t1l))
    copies = []
    for c in range(comps):
        for k in range(lanes):
            at = slice(128 * k, 128 * k + 128)
            done = done_ref.at[c, k]
            done[...] = even_ref[c, k]
            for y in range(8):
                done[pl.ds(16 * y, 8, stride=2)] = window[64 * c + 8 * y : 64 * c + 8 * y + 8, at]
            if 128 * k < quarter:
                for y in range(4):
                    done[pl.ds(32 * y, 4, stride=4)] = deepest[c][4 * y : 4 * y + 4, at]
            for y in range(8):
                copies.append(
                    pltpu.make_async_copy(done.at[pl.ds(16 * y, 16)], out_ref.at[c, pl.ds(32 * y, 16), at], sems.at[c])
                )
                copies[-1].start()
    for copy in copies:
        copy.wait()


def call(body, ins, outs, scratch=(), flops=0, hbm_in=(), hbm_out=(), aliases=None):
    def spec(n, hbm):
        return pl.BlockSpec(memory_space=pltpu.HBM if n in hbm else pltpu.VMEM)

    moved = sum(a.size * a.dtype.itemsize for a in ins)
    moved += sum(int(np.prod(s)) * jnp.dtype(d).itemsize for s, d in outs)
    return pl.pallas_call(
        body,
        in_specs=[spec(n, hbm_in) for n in range(len(ins))],
        out_specs=[spec(n, hbm_out) for n in range(len(outs))],
        out_shape=[jax.ShapeDtypeStruct(s, d) for s, d in outs],
        scratch_shapes=list(scratch),
        input_output_aliases=aliases or {},
        compiler_params=pltpu.CompilerParams(vmem_limit_bytes=VMEM_LIMIT),
        cost_estimate=pl.CostEstimate(flops=flops, bytes_accessed=moved, transcendentals=0),
    )(*ins)


def move(value, axis, step):
    count = lax.axis_size(axis)
    return lax.ppermute(value, axis, [(i, (i + step) % count) for i in range(count)])


def local(flow_field):
    comps, ny, nz, nx = flow_field.shape
    assert ny == ROWS and nz == ROWS and nx % 1024 == 0
    assert lax.axis_size("gy") >= 5 and lax.axis_size("gz") >= 5
    half, quarter, lanes = nx // 2, nx // 4, nx // 128
    pairs = {k: [jnp.asarray(p) for p in v] for k, v in tables(nx).items()}
    field = pltpu.with_memory_space_constraint(flow_field, pltpu.HBM)
    flat = pltpu.with_memory_space_constraint(flow_field.reshape(comps, ROWS * ROWS, nx), pltpu.HBM)

    def consts(*names):
        return [p for n in names for p in pairs[n]]

    def dma(*shape):
        return pltpu.SemaphoreType.DMA(shape)

    edge = ((comps, 2, ROWS, nx), F32)
    y_right, y_left, head = call(
        edge_kernel,
        [field],
        [edge] * 2 + [((ROWS, ROWS, nx), F32)],
        [pltpu.VMEM((comps, 7, ROWS, nx), F32), dma(comps, 2), pltpu.SemaphoreType.DMA],
        hbm_in=(0,),
    )
    from_left0 = move(y_right, "gy", 1)
    from_right0 = move(y_left, "gy", -1)

    near = ((comps, 64, half), F32)
    far = ((comps, 16, half), F32)
    cells = ((comps, lanes, ROWS * ROWS, 128), F32)
    u, first, second, z_right, z_left, z_right2, z_left2 = call(
        lift_kernel,
        [flat, head.reshape(ROWS * ROWS, nx)] + consts("tx", "rims", "zsend", "tx12"),
        [cells, ((comps, 112, half), F32), ((comps, 64, quarter), F32)] + [near] * 2 + [far] * 2,
        [
            pltpu.VMEM((comps, ROWS * ROWS, nx), F32),
            pltpu.VMEM((ROWS * ROWS, half), BF16),
            pltpu.VMEM((ROWS * ROWS, half), BF16),
            pltpu.VMEM((comps, 192, half), F32),
            dma(comps),
        ],
        flops=1 << 33,
        hbm_in=(0,),
    )
    z_from_left2 = move(z_right2, "gz", 2)
    z_from_left = move(z_right, "gz", 1)
    z_from_right = move(z_left, "gz", -1)
    z_from_right2 = move(z_left2, "gz", -2)

    planes = ((comps, lanes, 2, ROWS, 128), F32)
    b, z0_right, z0_left = call(
        along_y_kernel,
        [z_from_left2, z_from_right2, u, from_left0, from_right0] + consts("tx", "rims"),
        [cells] + [planes] * 2,
        [pltpu.VMEM((lanes, 64 * comps, 128), F32)],
        flops=1 << 32,
    )
    z0_from_left = move(z0_right, "gz", 1)
    z0_from_right = move(z0_left, "gz", -1)

    o1, o2, y1_right, y1_left, away = call(
        chain_kernel,
        [first, second, z_from_left, z_from_right, z_from_left2, z_from_right2] + consts("chain1", "chain2", "tx12"),
        [((comps, 64, half), F32), ((comps, 16, quarter), F32)]
        + [((comps, 32, half), F32)] * 2
        + [((comps, 16, quarter), F32)],
        [pltpu.VMEM((comps, 64, half), F32)],
        flops=1 << 31,
    )
    y_from_left = move(y1_right, "gy", 1)
    y_from_right = move(y1_left, "gy", -1)
    y2_right, y2_left = call(away_kernel, [z0_from_left, away], [((comps, 8, quarter), F32)] * 2)
    y_from_left2 = move(y2_right, "gy", 2)
    y_from_right2 = move(y2_left, "gy", -2)

    whole = ((comps, ROWS * ROWS, nx), F32)
    result, even = call(
        along_z_kernel,
        [b, z0_from_left, z0_from_right],
        [whole, ((comps, lanes // 2, ROWS * ROWS // 2, 128), F32)],
        [pltpu.VMEM((comps, lanes, ROWS * ROWS, 128), F32), dma(comps)],
        flops=1 << 32,
        hbm_out=(0,),
    )
    (result,) = call(
        last_kernel,
        [result, even, o1, o2, y_from_left, y_from_right, y_from_left2, y_from_right2]
        + consts("ygive1", "ygive2", "tx1"),
        [whole],
        [pltpu.VMEM((comps, lanes // 2, ROWS * ROWS // 2, 128), F32), dma(comps)],
        flops=1 << 30,
        hbm_in=(0,),
        hbm_out=(0,),
        aliases={0: 0},
    )
    return result.reshape(flow_field.shape)


def solution(mesh):
    placed = P(None, "gy", "gz", None)
    return jax.shard_map(local, mesh=mesh, in_specs=(placed,), out_specs=placed, check_vma=False)
```

```python
import jax
import jax.numpy as jnp
import ml_dtypes
import numpy as np
from jax import lax
from jax.experimental import pallas as pl
from jax.experimental.pallas import tpu as pltpu
from jax.sharding import PartitionSpec as P

ALPHA = -1.586134342059924
BETA = -0.052980118572961
GAMMA = 0.882911075530934
DELTA = 0.443506852043971
KAPPA = 1.149604398860241

F32 = jnp.float32
BF16 = jnp.bfloat16
VMEM_LIMIT = 32 * 1024 * 1024
ROWS = 16


def pair_matrix(length):
    cells = np.eye(length)
    even, odd = cells[0::2].copy(), cells[1::2].copy()
    odd = odd + ALPHA * (even + np.roll(even, -1, 0))
    even = even + BETA * (odd + np.roll(odd, 1, 0))
    odd = odd + GAMMA * (even + np.roll(even, -1, 0))
    even = even + DELTA * (odd + np.roll(odd, 1, 0))
    return even * KAPPA, odd / KAPPA


def alternated(length):
    low, high = pair_matrix(length)
    table = np.zeros((length, length))
    table[0::2], table[1::2] = low, high
    return table


def chain_blocks():
    count = 8
    length = count * ROWS
    first = alternated(length)
    second = alternated(length // 2) @ first[0::2]
    third = alternated(length // 4) @ second[0::2]
    result = []
    for table, per in ((first, 16), (second, 8), (third, 4)):
        here = table[4 * per : 5 * per]
        result.append({k: here[:, (4 + k) * ROWS : (5 + k) * ROWS] for k in (-2, -1, 0, 1, 2)})
    return result


def factor(block, rank):
    left, size, right = np.linalg.svd(block, full_matrices=False)
    assert np.all(size[rank:] < 1e-12)
    return left[:, :rank] * size[:rank], right[:rank]


def split_const(table):
    table = np.asarray(table, np.float64)
    high = table.astype(ml_dtypes.bfloat16)
    low = (table - high.astype(np.float64)).astype(ml_dtypes.bfloat16)
    return high, low


def stack(*parts):
    return np.concatenate(parts, 0)


def tables(nx):
    first, second, third = chain_blocks()
    eye = np.eye
    sides = (-1, 1)
    out = {}
    give1, send1, give2a, give2b, send2 = {}, {}, {}, {}, {}
    give2, send2d, give22, send22 = {}, {}, {}, {}
    for s in sides:
        give1[s], send1[s] = factor(second[s], 3)
        give2a[s] = third[s] @ send1[s].T
        give2b[s], send2[s] = factor(third[s] - give2a[s] @ send1[s], 2)
        give2[s], send2d[s] = factor(third[s], 4)
        give22[s], send22[s] = factor(third[2 * s], 2)

    low, high = pair_matrix(nx)
    out["tx"] = np.concatenate([low[128:256, 256:512], high[128:256, 256:512]], 0).T
    blocks = nx // 256
    rims = np.zeros((8 * blocks, nx))
    for j in range(blocks):
        block = np.concatenate([low[128 * j : 128 * j + 128], high[128 * j : 128 * j + 128]], 0).T
        after = (j + 1) % blocks
        rims[8 * j : 8 * j + 4, 256 * j : 256 * j + 256] = block[(256 * j - np.arange(4, 0, -1)) % nx]
        rims[8 * after + 4 : 8 * after + 8, 256 * j : 256 * j + 256] = block[256 * after : 256 * after + 4]
    low, high = pair_matrix(nx // 2)
    tx1 = np.concatenate([low, high], 0).T
    low, high = pair_matrix(nx // 4)
    tx2 = np.concatenate([low, high], 0).T
    out["tx1"] = tx1
    out["tx12"] = tx1[:, : nx // 4] @ tx2

    def planes(send):
        return np.einsum("pz,ab->paBz".replace("B", "b"), send, eye(ROWS)).reshape(-1, ROWS * ROWS)

    zsend = [planes(send[s]) for send in (send1, send2, send22) for s in sides]

    def back(give):
        return np.einsum("zp,ab->azpb", give, eye(ROWS)).reshape(ROWS * give.shape[0], -1)

    zgive1 = np.concatenate([back(give1[s]) for s in sides], 1)
    zgive2a = np.concatenate([back(give2a[s]) for s in sides], 1)
    zgive2b = np.concatenate([back(give2b[s]) for s in sides] + [back(give22[s]) for s in sides], 1)
    ychain1 = stack(np.kron(second[0], eye(8)), *[np.kron(send1[s], eye(8)) for s in sides])
    ychain2 = stack(
        np.kron(third[0], eye(4)),
        *[np.kron(send2d[s], eye(4)) for s in sides],
        *[np.kron(send22[s], eye(4)) for s in sides],
    )
    own1, own2 = np.kron(eye(ROWS), second[0]), np.kron(eye(ROWS), third[0])
    out["zsend"] = stack(*zsend, ychain2 @ own2, ychain1 @ own1)
    out["chain1"] = stack(ychain1 @ zgive1, ychain2 @ zgive2a)
    out["chain2"] = ychain2 @ zgive2b
    out["ygive1"] = np.concatenate([np.kron(give1[s], eye(8)) for s in sides], 1)
    out["ygive2"] = np.concatenate(
        [np.kron(give2[s], eye(4)) for s in sides] + [np.kron(give22[s], eye(4)) for s in sides], 1
    )
    pairs = {name: split_const(table) for name, table in out.items()}
    high, low = split_const(rims)
    pairs["rims"] = (np.concatenate([high, high, low, np.zeros_like(high)], 0),)
    return pairs


def split(value):
    high = value.astype(BF16)
    low = (value - high.astype(F32)).astype(BF16)
    return high, low


def dot(a, b):
    return jnp.dot(a, b, preferred_element_type=F32)


def left(table, rows):
    return dot(table[0], rows[0]) + (dot(table[0], rows[1]) + dot(table[1], rows[0]))


def right(rows, table):
    return dot(rows[0], table[0]) + (dot(rows[0], table[1]) + dot(rows[1], table[0]))


def both(high_ref, low_ref):
    return high_ref[...], low_ref[...]


def lift_line(cells, before, after):
    even, odd = list(cells[0::2]), list(cells[1::2])
    count = len(even)
    even.append(after[0])
    odd = [odd[n] + ALPHA * (even[n] + even[n + 1]) for n in range(count)]
    odd_before = before[0] + ALPHA * even[0]
    even_before = before[1] + BETA * odd_before
    odd_around = [odd_before] + odd + [after[1]]
    even = [even[n] + BETA * (odd_around[n + 1] + odd_around[n]) for n in range(count + 1)]
    odd = [odd[n] + GAMMA * (even[n] + even[n + 1]) for n in range(count)]
    odd_around = [odd_before + GAMMA * (even_before + even[0])] + odd
    even = [even[n] + DELTA * (odd_around[n + 1] + odd_around[n]) for n in range(count)]
    result = []
    for n in range(count):
        result += [even[n] * KAPPA, odd[n] * (1.0 / KAPPA)]
    return result


def give_right(cells):
    a, b, c, d = cells
    return d + ALPHA * c, c + BETA * (b + ALPHA * (a + c))


def give_left(cells):
    a, b, c = cells
    return a, b + ALPHA * (a + c)


def lift_x(cells, table, rims_ref, store):
    count, nx = cells.shape
    lane = lax.broadcasted_iota(jnp.int32, (count, 128), 1)
    rims = None
    for j in range(nx // 256):
        at = 256 * j
        before = cells[:, nx - 128 :] if j == 0 else cells[:, at - 128 : at]
        rim = jnp.where(lane >= 124, before, jnp.where(lane < 4, cells[:, at : at + 128], 0.0))
        rim = pltpu.roll(rim, 4 + 8 * j, 1)
        rims = rim if rims is None else rims + rim
    width = nx // 32
    high = rims.astype(BF16).astype(F32)
    rims = (high + pltpu.roll(rims - high, width, 1) + pltpu.roll(high, 2 * width, 1)).astype(BF16)
    parts = split(cells)
    for j in range(nx // 256):
        lanes = slice(256 * j, 256 * j + 256)
        store(j, right([part[:, lanes] for part in parts], table) + dot(rims, rims_ref[:, lanes]))


def edge_kernel(x_ref, to_right_ref, to_left_ref, head_ref, rows_ref, sems, head_sem):
    comps = x_ref.shape[0]
    copies = []
    for c in range(comps):
        copies.append(pltpu.make_async_copy(x_ref.at[c, pl.ds(0, 3)], rows_ref.at[c, pl.ds(0, 3)], sems.at[c, 0]))
        copies.append(pltpu.make_async_copy(x_ref.at[c, pl.ds(12, 4)], rows_ref.at[c, pl.ds(3, 4)], sems.at[c, 1]))
    head = pltpu.make_async_copy(x_ref.at[0], head_ref, head_sem)
    for copy in copies:
        copy.start()
    head.start()
    for c in range(comps):
        copies[2 * c].wait()
        to_left_ref[c, 0], to_left_ref[c, 1] = give_left([rows_ref[c, k] for k in range(3)])
        copies[2 * c + 1].wait()
        to_right_ref[c, 0], to_right_ref[c, 1] = give_right([rows_ref[c, k] for k in range(3, 7)])
    head.wait()


def lift_kernel(
    x_ref, head_ref, txh, txl, rims, zsh, zsl, t12h, t12l,
    u_ref, first_ref, second_ref, r1_ref, l1_ref, r2_ref, l2_ref, cells_ref, high_ref, low_ref, far_ref, sems,
):
    comps, _, nx = x_ref.shape
    blocks, quarter = nx // 256, nx // 4

    def copy(c):
        return pltpu.make_async_copy(x_ref.at[c], cells_ref.at[c], sems.at[c])

    for c in range(1, comps):
        copy(c).start()

    def part(c, cells):
        def store(j, value):
            u_ref[c, j] = value[:, :128]
            u_ref[c, blocks + j] = value[:, 128:]
            high, low = split(value[:, :128])
            high_ref[:, 128 * j : 128 * j + 128] = high
            low_ref[:, 128 * j : 128 * j + 128] = low

        lift_x(cells, both(txh, txl), rims, store)
        rows = left(both(zsh, zsl), both(high_ref, low_ref))
        r1_ref[c, :48] = rows[:48]
        l1_ref[c, :48] = rows[48:96]
        far_ref[c] = rows[96:288]
        first_ref[c] = rows[288:]

    def step(c, _):
        copy(c).wait()
        part(c, cells_ref[c])
        return 0

    part(0, head_ref[...])
    lax.fori_loop(1, comps, step, 0, unroll=True)
    far = right(split(far_ref[...].reshape(192 * comps, nx // 2)), both(t12h, t12l))
    for c in range(comps):
        for k, (ref, ref2) in enumerate(((r1_ref, r2_ref), (l1_ref, l2_ref))):
            for p in range(2):
                lanes = slice(quarter * p, quarter * p + quarter)
                at = 192 * c + 32 * k + 16 * p
                ref[c, 48:, lanes] = far[at : at + 16]
                ref2[c, :, lanes] = far[at + 64 : at + 80]
        second_ref[c] = far[192 * c + 128 : 192 * c + 192]


def chain_kernel(
    first_ref, second_ref, l1_ref, r1_ref, l2_ref, r2_ref,
    g1h, g1l, g2h, g2l, t12h, t12l,
    o1_ref, o2_ref, to_r_ref, to_l_ref, to_r2_ref, to_l2_ref, far_ref,
):
    comps, _, half = first_ref.shape
    quarter = half // 2

    def step(c, _):
        near = split(jnp.concatenate([l1_ref[c, :48], r1_ref[c, :48]], 0))
        rows = left(both(g1h, g1l), near)
        far_ref[c] = rows[112:]
        first = first_ref[c] + rows[:112]
        o1_ref[c] = first[:64]
        to_r_ref[c, :24] = first[64:88]
        to_l_ref[c, :24] = first[88:]
        return 0

    lax.fori_loop(0, comps, step, 0)
    far = right(split(far_ref[...].reshape(64 * comps, half)), both(t12h, t12l))
    for c in range(comps):
        deep = []
        for ref in (l1_ref, r1_ref):
            deep += [ref[c, 48:, :quarter], ref[c, 48:, quarter:]]
        for ref in (l2_ref, r2_ref):
            deep += [ref[c, :, :quarter], ref[c, :, quarter:]]
        second = left(both(g2h, g2l), split(jnp.concatenate(deep, 0)))
        second = second_ref[c] + (far[64 * c : 64 * c + 64] + second)
        o2_ref[c] = second[:16]
        for k, ref in enumerate((to_r_ref, to_l_ref)):
            ref[c, 24:, :quarter] = second[16 + 16 * k : 24 + 16 * k]
            ref[c, 24:, quarter:] = second[24 + 16 * k : 32 + 16 * k]
        to_r2_ref[c] = second[48:56]
        to_l2_ref[c] = second[56:]


def along_y_kernel(u_ref, b_ref):
    comps, lanes = u_ref.shape[:2]

    def step(n, _):
        c, k = n // lanes, n % lanes
        u, b = u_ref.at[c, k], b_ref.at[c, k]
        nothing = [jnp.zeros((8, 128), F32)] * 2
        for part in range(2):
            cells = [u[16 * y + 8 * part : 16 * y + 8 * part + 8] for y in range(ROWS)]
            for y, value in enumerate(lift_line(cells, nothing, nothing)):
                b[pl.ds(128 * part + y, 8, stride=ROWS)] = value
        return 0

    lax.fori_loop(0, comps * lanes, step, 0, unroll=2)


def rim_kernel(_, _2, own_ref, l_ref, r_ref, txh, txl, rims, b_ref, to_r_ref, to_l_ref, halo_ref, added_ref):
    comps, lanes = own_ref.shape[:2]
    blocks = lanes // 2

    def store(j, value):
        halo_ref[j] = value[:, :128]
        halo_ref[blocks + j] = value[:, 128:]

    rows = [ref[c, p] for c in range(comps) for ref in (l_ref, r_ref) for p in range(2)]
    lift_x(jnp.concatenate(rows, 0), both(txh, txl), rims, store)
    added_ref[...] = jnp.zeros_like(added_ref)
    units = np.eye(4)
    weights = np.array([lift_line([0.0] * ROWS, list(unit[:2]), list(unit[2:])) for unit in units])

    def step(n, _):
        c, k = n // lanes, n % lanes
        b, halo, added = b_ref.at[c, k], halo_ref.at[k], added_ref.at[n % 2]
        for part in range(2):
            around = [halo[pl.ds(pl.multiple_of(64 * c + 16 * p + 8 * part, 8), 8)] for p in range(4)]
            for y in range(ROWS):
                terms = [float(weights[p, y]) * around[p] for p in range(4) if weights[p, y] != 0.0]
                if terms:
                    added[pl.ds(128 * part + y, 8, stride=ROWS)] = sum(terms[1:], terms[0])
        for z in range(ROWS):
            at = slice(16 * z, 16 * z + 16)
            b[at] = own_ref[c, k, at] + added[at]

        def plane(z):
            return own_ref[c, k, 16 * z : 16 * z + 16] + added[16 * z : 16 * z + 16]

        to_r_ref[c, k, 0], to_r_ref[c, k, 1] = give_right([plane(z) for z in range(12, 16)])
        to_l_ref[c, k, 0], to_l_ref[c, k, 1] = give_left([plane(z) for z in range(3)])
        return 0

    lax.fori_loop(0, comps * lanes, step, 0, unroll=2)


def hand_on_kernel(_, value_ref, out_ref):
    out_ref[...] = value_ref[...]


def along_z_kernel(b_ref, l_ref, r_ref, out_ref, even_ref, done_ref, sems):
    comps, lanes = b_ref.shape[:2]

    def copy(c, k):
        return pltpu.make_async_copy(
            done_ref.at[c, k], out_ref.at[c, :, pl.ds(pl.multiple_of(128 * k, 128), 128)], sems.at[c]
        )

    def step(n, _):
        c, k = n // lanes, n % lanes
        b, done = b_ref.at[c, k], done_ref.at[c, k]
        for part in range(2):
            cells = [b[16 * z + 8 * part : 16 * z + 8 * part + 8] for z in range(ROWS)]
            around = [ref[c, k, p, 8 * part : 8 * part + 8] for ref in (l_ref, r_ref) for p in range(2)]
            for z, value in enumerate(lift_line(cells, around[:2], around[2:])):
                done[pl.ds(128 * part + z, 8, stride=ROWS)] = value
        copy(c, k).start()

        @pl.when(k < lanes // 2)
        def _():
            for y in range(ROWS // 2):
                even_ref[c, k, y] = done[32 * y : 32 * y + 16]

        return 0

    lax.fori_loop(0, comps * lanes, step, 0, unroll=2)
    for c in range(comps):
        for k in range(lanes):
            copy(c, k).wait()


def last_kernel(
    _, even_ref, o1_ref, o2_ref, l1_ref, r1_ref, l2_ref, r2_ref,
    g1h, g1l, g2h, g2l, t1h, t1l, out_ref, done_ref, sems,
):
    comps, lanes = even_ref.shape[:2]
    half = 128 * lanes
    quarter = half // 2
    window, deepest = [], []
    for c in range(comps):
        near = split(jnp.concatenate([l1_ref[c, :24], r1_ref[c, :24]], 0))
        window.append(o1_ref[c] + left(both(g1h, g1l), near))
        deep = []
        for ref in (l1_ref, r1_ref):
            deep += [ref[c, 24:, :quarter], ref[c, 24:, quarter:]]
        deep += [l2_ref[c], r2_ref[c]]
        deepest.append(o2_ref[c] + left(both(g2h, g2l), split(jnp.concatenate(deep, 0))))
    window = right(split(jnp.concatenate(window, 0)), both(t1h, t1l))
    copies = []
    for c in range(comps):
        for k in range(lanes):
            at = slice(128 * k, 128 * k + 128)
            for y in range(8):
                done_ref[c, k, y] = even_ref[c, k, y]
                done_ref[c, k, y, pl.ds(0, 8, stride=2)] = window[64 * c + 8 * y : 64 * c + 8 * y + 8, at]
            if 128 * k < quarter:
                for y in range(4):
                    done_ref[c, k, 2 * y, pl.ds(0, 4, stride=4)] = deepest[c][4 * y : 4 * y + 4, at]
            copies.append(pltpu.make_async_copy(done_ref.at[c, k], out_ref.at[c, :, 0, :, at], sems.at[c]))
            copies[-1].start()
    for copy in copies:
        copy.wait()


def call(body, ins, outs, scratch=(), flops=0, hbm_in=(), hbm_out=(), aliases=None):
    def spec(n, hbm):
        return pl.BlockSpec(memory_space=pltpu.HBM if n in hbm else pltpu.VMEM)

    moved = sum(a.size * a.dtype.itemsize for a in ins)
    moved += sum(int(np.prod(s)) * jnp.dtype(d).itemsize for s, d in outs)
    return pl.pallas_call(
        body,
        in_specs=[spec(n, hbm_in) for n in range(len(ins))],
        out_specs=[spec(n, hbm_out) for n in range(len(outs))],
        out_shape=[jax.ShapeDtypeStruct(s, d) for s, d in outs],
        scratch_shapes=list(scratch),
        input_output_aliases=aliases or {},
        compiler_params=pltpu.CompilerParams(vmem_limit_bytes=VMEM_LIMIT),
        cost_estimate=pl.CostEstimate(flops=flops, bytes_accessed=moved, transcendentals=0),
    )(*ins)


def move(value, axis, step):
    count = lax.axis_size(axis)
    return lax.ppermute(value, axis, [(i, (i + step) % count) for i in range(count)])


def local(flow_field):
    comps, ny, nz, nx = flow_field.shape
    assert ny == ROWS and nz == ROWS and nx % 1024 == 0
    assert lax.axis_size("gy") >= 5 and lax.axis_size("gz") >= 5
    half, quarter, lanes = nx // 2, nx // 4, nx // 128
    pairs = {k: [jnp.asarray(p) for p in v] for k, v in tables(nx).items()}
    field = pltpu.with_memory_space_constraint(flow_field, pltpu.HBM)
    flat = pltpu.with_memory_space_constraint(flow_field.reshape(comps, ROWS * ROWS, nx), pltpu.HBM)

    def consts(*names):
        return [p for n in names for p in pairs[n]]

    def dma(*shape):
        return pltpu.SemaphoreType.DMA(shape)

    edge = ((comps, 2, ROWS, nx), F32)
    y_right, y_left, head = call(
        edge_kernel,
        [field],
        [edge] * 2 + [((ROWS, ROWS, nx), F32)],
        [pltpu.VMEM((comps, 7, ROWS, nx), F32), dma(comps, 2), pltpu.SemaphoreType.DMA],
        hbm_in=(0,),
    )
    from_left0 = move(y_right, "gy", 1)
    from_right0 = move(y_left, "gy", -1)

    near = ((comps, 64, half), F32)
    far = ((comps, 16, half), F32)
    cells = ((comps, lanes, ROWS * ROWS, 128), F32)
    u, first, second, z_right, z_left, z_right2, z_left2 = call(
        lift_kernel,
        [flat, head.reshape(ROWS * ROWS, nx)] + consts("tx", "rims", "zsend", "tx12"),
        [cells, ((comps, 112, half), F32), ((comps, 64, quarter), F32)] + [near] * 2 + [far] * 2,
        [
            pltpu.VMEM((comps, ROWS * ROWS, nx), F32),
            pltpu.VMEM((ROWS * ROWS, half), BF16),
            pltpu.VMEM((ROWS * ROWS, half), BF16),
            pltpu.VMEM((comps, 192, half), F32),
            dma(comps),
        ],
        flops=1 << 33,
        hbm_in=(0,),
    )
    z_from_left2 = move(z_right2, "gz", 2)
    z_from_left = move(z_right, "gz", 1)
    z_from_right = move(z_left, "gz", -1)
    z_from_right2 = move(z_left2, "gz", -2)

    planes = ((comps, lanes, 2, ROWS, 128), F32)
    (own,) = call(along_y_kernel, [u], [cells], flops=1 << 31)
    b, z0_right, z0_left = call(
        rim_kernel,
        [z_from_left2, z_from_right2, own, from_left0, from_right0] + consts("tx", "rims"),
        [cells] + [planes] * 2,
        [pltpu.VMEM((lanes, 64 * comps, 128), F32), pltpu.VMEM((2, ROWS * ROWS, 128), F32)],
        flops=1 << 31,
    )
    z0_from_left = move(z0_right, "gz", 1)
    z0_from_right = move(z0_left, "gz", -1)

    o1, o2, y1_right, y1_left, y2_right, y2_left = call(
        chain_kernel,
        [first, second, z_from_left, z_from_right, z_from_left2, z_from_right2] + consts("chain1", "chain2", "tx12"),
        [((comps, 64, half), F32), ((comps, 16, quarter), F32)]
        + [((comps, 32, half), F32)] * 2
        + [((comps, 8, quarter), F32)] * 2,
        [pltpu.VMEM((comps, 64, half), F32)],
        flops=1 << 31,
    )
    y_from_left = move(y1_right, "gy", 1)
    y_from_left2 = move(y2_right, "gy", 2)
    (y1_left,) = call(hand_on_kernel, [z0_from_left, y1_left], [((comps, 32, half), F32)])
    (y2_left,) = call(hand_on_kernel, [z0_from_right, y2_left], [((comps, 8, quarter), F32)])
    y_from_right = move(y1_left, "gy", -1)
    y_from_right2 = move(y2_left, "gy", -2)

    whole = ((comps, ROWS * ROWS, nx), F32)
    result, even = call(
        along_z_kernel,
        [b, z0_from_left, z0_from_right],
        [whole, ((comps, lanes // 2, 8, ROWS, 128), F32)],
        [pltpu.VMEM((comps, lanes, ROWS * ROWS, 128), F32), dma(comps)],
        flops=1 << 32,
        hbm_out=(0,),
    )
    pairs_of_rows = ((comps, 8, 2, ROWS, nx), F32)
    (result,) = call(
        last_kernel,
        [result.reshape(pairs_of_rows[0]), even, o1, o2, y_from_left, y_from_right, y_from_left2, y_from_right2]
        + consts("ygive1", "ygive2", "tx1"),
        [pairs_of_rows],
        [pltpu.VMEM((comps, lanes // 2, 8, ROWS, 128), F32), dma(comps)],
        flops=1 << 30,
        hbm_in=(0,),
        hbm_out=(0,),
        aliases={0: 0},
    )
    return result.reshape(flow_field.shape)


def solution(mesh):
    placed = P(None, "gy", "gz", None)
    return jax.shard_map(local, mesh=mesh, in_specs=(placed,), out_specs=placed, check_vma=False)
```

```python
import jax
import jax.numpy as jnp
import ml_dtypes
import numpy as np
from jax import lax
from jax.experimental import pallas as pl
from jax.experimental.pallas import tpu as pltpu
from jax.sharding import PartitionSpec as P

ALPHA = -1.586134342059924
BETA = -0.052980118572961
GAMMA = 0.882911075530934
DELTA = 0.443506852043971
KAPPA = 1.149604398860241

F32 = jnp.float32
BF16 = jnp.bfloat16
VMEM_LIMIT = 32 * 1024 * 1024
ROWS = 16


def pair_matrix(length):
    cells = np.eye(length)
    even, odd = cells[0::2].copy(), cells[1::2].copy()
    odd = odd + ALPHA * (even + np.roll(even, -1, 0))
    even = even + BETA * (odd + np.roll(odd, 1, 0))
    odd = odd + GAMMA * (even + np.roll(even, -1, 0))
    even = even + DELTA * (odd + np.roll(odd, 1, 0))
    return even * KAPPA, odd / KAPPA


def alternated(length):
    low, high = pair_matrix(length)
    table = np.zeros((length, length))
    table[0::2], table[1::2] = low, high
    return table


def chain_blocks():
    count = 8
    length = count * ROWS
    first = alternated(length)
    second = alternated(length // 2) @ first[0::2]
    third = alternated(length // 4) @ second[0::2]
    result = []
    for table, per in ((first, 16), (second, 8), (third, 4)):
        here = table[4 * per : 5 * per]
        result.append({k: here[:, (4 + k) * ROWS : (5 + k) * ROWS] for k in (-2, -1, 0, 1, 2)})
    return result


def factor(block, rank):
    left, size, right = np.linalg.svd(block, full_matrices=False)
    assert np.all(size[rank:] < 1e-12)
    return left[:, :rank] * size[:rank], right[:rank]


def split_const(table):
    table = np.asarray(table, np.float64)
    high = table.astype(ml_dtypes.bfloat16)
    low = (table - high.astype(np.float64)).astype(ml_dtypes.bfloat16)
    return high, low


def stack(*parts):
    return np.concatenate(parts, 0)


def tables(nx):
    first, second, third = chain_blocks()
    eye = np.eye
    sides = (-1, 1)
    out = {}
    give1, send1, give2a, give2b, send2 = {}, {}, {}, {}, {}
    give2, send2d, give22, send22 = {}, {}, {}, {}
    for s in sides:
        give1[s], send1[s] = factor(second[s], 3)
        give2a[s] = third[s] @ send1[s].T
        give2b[s], send2[s] = factor(third[s] - give2a[s] @ send1[s], 2)
        give2[s], send2d[s] = factor(third[s], 4)
        give22[s], send22[s] = factor(third[2 * s], 2)

    low, high = pair_matrix(nx)
    out["tx"] = np.concatenate([low[128:256, 256:512], high[128:256, 256:512]], 0).T
    blocks = nx // 256
    rims = np.zeros((8 * blocks, nx))
    for j in range(blocks):
        block = np.concatenate([low[128 * j : 128 * j + 128], high[128 * j : 128 * j + 128]], 0).T
        after = (j + 1) % blocks
        rims[8 * j : 8 * j + 4, 256 * j : 256 * j + 256] = block[(256 * j - np.arange(4, 0, -1)) % nx]
        rims[8 * after + 4 : 8 * after + 8, 256 * j : 256 * j + 256] = block[256 * after : 256 * after + 4]
    low, high = pair_matrix(nx // 2)
    tx1 = np.concatenate([low, high], 0).T
    low, high = pair_matrix(nx // 4)
    tx2 = np.concatenate([low, high], 0).T
    out["tx1"] = tx1
    out["tx12"] = tx1[:, : nx // 4] @ tx2

    def planes(send):
        return np.einsum("pz,ab->paBz".replace("B", "b"), send, eye(ROWS)).reshape(-1, ROWS * ROWS)

    zsend = [planes(send[s]) for send in (send1, send2, send22) for s in sides]

    def back(give):
        return np.einsum("zp,ab->azpb", give, eye(ROWS)).reshape(ROWS * give.shape[0], -1)

    zgive1 = np.concatenate([back(give1[s]) for s in sides], 1)
    zgive2a = np.concatenate([back(give2a[s]) for s in sides], 1)
    zgive2b = np.concatenate([back(give2b[s]) for s in sides] + [back(give22[s]) for s in sides], 1)
    ychain1 = stack(np.kron(second[0], eye(8)), *[np.kron(send1[s], eye(8)) for s in sides])
    ychain2 = stack(
        np.kron(third[0], eye(4)),
        *[np.kron(send2d[s], eye(4)) for s in sides],
        *[np.kron(send22[s], eye(4)) for s in sides],
    )
    own1, own2 = np.kron(eye(ROWS), second[0]), np.kron(eye(ROWS), third[0])
    out["zsend"] = stack(*zsend, ychain2 @ own2, ychain1 @ own1)
    out["chain1"] = stack(ychain1 @ zgive1, ychain2 @ zgive2a)
    out["chain2"] = ychain2 @ zgive2b
    out["ygive1"] = np.concatenate([np.kron(give1[s], eye(8)) for s in sides], 1)
    out["ygive2"] = np.concatenate(
        [np.kron(give2[s], eye(4)) for s in sides] + [np.kron(give22[s], eye(4)) for s in sides], 1
    )
    pairs = {name: split_const(table) for name, table in out.items()}
    high, low = split_const(rims)
    pairs["rims"] = (np.concatenate([high, high, low, np.zeros_like(high)], 0),)
    return pairs


def split(value):
    high = value.astype(BF16)
    low = (value - high.astype(F32)).astype(BF16)
    return high, low


def dot(a, b):
    return jnp.dot(a, b, preferred_element_type=F32)


def left(table, rows):
    return dot(table[0], rows[0]) + (dot(table[0], rows[1]) + dot(table[1], rows[0]))


def right(rows, table):
    return dot(rows[0], table[0]) + (dot(rows[0], table[1]) + dot(rows[1], table[0]))


def both(high_ref, low_ref):
    return high_ref[...], low_ref[...]


def lift_line(cells, before, after):
    even, odd = list(cells[0::2]), list(cells[1::2])
    count = len(even)
    even.append(after[0])
    odd = [odd[n] + ALPHA * (even[n] + even[n + 1]) for n in range(count)]
    odd_before = before[0] + ALPHA * even[0]
    even_before = before[1] + BETA * odd_before
    odd_around = [odd_before] + odd + [after[1]]
    even = [even[n] + BETA * (odd_around[n + 1] + odd_around[n]) for n in range(count + 1)]
    odd = [odd[n] + GAMMA * (even[n] + even[n + 1]) for n in range(count)]
    odd_around = [odd_before + GAMMA * (even_before + even[0])] + odd
    even = [even[n] + DELTA * (odd_around[n + 1] + odd_around[n]) for n in range(count)]
    result = []
    for n in range(count):
        result += [even[n] * KAPPA, odd[n] * (1.0 / KAPPA)]
    return result


def give_right(cells):
    a, b, c, d = cells
    return d + ALPHA * c, c + BETA * (b + ALPHA * (a + c))


def give_left(cells):
    a, b, c = cells
    return a, b + ALPHA * (a + c)


def lift_x(cells, table, rims_ref, store):
    count, nx = cells.shape
    lane = lax.broadcasted_iota(jnp.int32, (count, 128), 1)
    rims = None
    for j in range(nx // 256):
        at = 256 * j
        before = cells[:, nx - 128 :] if j == 0 else cells[:, at - 128 : at]
        rim = jnp.where(lane >= 124, before, jnp.where(lane < 4, cells[:, at : at + 128], 0.0))
        rim = pltpu.roll(rim, 4 + 8 * j, 1)
        rims = rim if rims is None else rims + rim
    width = nx // 32
    high = rims.astype(BF16).astype(F32)
    rims = (high + pltpu.roll(rims - high, width, 1) + pltpu.roll(high, 2 * width, 1)).astype(BF16)
    parts = split(cells)
    for j in range(nx // 256):
        lanes = slice(256 * j, 256 * j + 256)
        store(j, right([part[:, lanes] for part in parts], table) + dot(rims, rims_ref[:, lanes]))


def edge_kernel(x_ref, to_right_ref, to_left_ref, head_ref, rows_ref, sems, head_sem):
    comps = x_ref.shape[0]
    copies = []
    for c in range(comps):
        copies.append(pltpu.make_async_copy(x_ref.at[c, pl.ds(0, 3)], rows_ref.at[c, pl.ds(0, 3)], sems.at[c, 0]))
        copies.append(pltpu.make_async_copy(x_ref.at[c, pl.ds(12, 4)], rows_ref.at[c, pl.ds(3, 4)], sems.at[c, 1]))
    head = pltpu.make_async_copy(x_ref.at[0], head_ref, head_sem)
    for copy in copies:
        copy.start()
    head.start()
    for c in range(comps):
        copies[2 * c].wait()
        to_left_ref[c, 0], to_left_ref[c, 1] = give_left([rows_ref[c, k] for k in range(3)])
        copies[2 * c + 1].wait()
        to_right_ref[c, 0], to_right_ref[c, 1] = give_right([rows_ref[c, k] for k in range(3, 7)])
    head.wait()


def lift_kernel(
    x_ref, head_ref, txh, txl, rims, zsh, zsl, t12h, t12l,
    u_ref, first_ref, second_ref, r1_ref, l1_ref, r2_ref, l2_ref, cells_ref, high_ref, low_ref, far_ref, sems,
):
    comps, _, nx = x_ref.shape
    blocks, quarter = nx // 256, nx // 4

    def copy(c):
        return pltpu.make_async_copy(x_ref.at[c], cells_ref.at[c], sems.at[c])

    for c in range(1, comps):
        copy(c).start()

    def part(c, cells):
        def store(j, value):
            u_ref[c, j] = value[:, :128]
            u_ref[c, blocks + j] = value[:, 128:]
            high, low = split(value[:, :128])
            high_ref[:, 128 * j : 128 * j + 128] = high
            low_ref[:, 128 * j : 128 * j + 128] = low

        lift_x(cells, both(txh, txl), rims, store)
        rows = left(both(zsh, zsl), both(high_ref, low_ref))
        r1_ref[c, :48] = rows[:48]
        l1_ref[c, :48] = rows[48:96]
        far_ref[c] = rows[96:288]
        first_ref[c] = rows[288:]

    def step(c, _):
        copy(c).wait()
        part(c, cells_ref[c])
        return 0

    part(0, head_ref[...])
    lax.fori_loop(1, comps, step, 0, unroll=True)
    far = right(split(far_ref[...].reshape(192 * comps, nx // 2)), both(t12h, t12l))
    for c in range(comps):
        for k, (ref, ref2) in enumerate(((r1_ref, r2_ref), (l1_ref, l2_ref))):
            for p in range(2):
                lanes = slice(quarter * p, quarter * p + quarter)
                at = 192 * c + 32 * k + 16 * p
                ref[c, 48:, lanes] = far[at : at + 16]
                ref2[c, :, lanes] = far[at + 64 : at + 80]
        second_ref[c] = far[192 * c + 128 : 192 * c + 192]


def chain_kernel(
    first_ref, second_ref, l1_ref, r1_ref, l2_ref, r2_ref,
    g1h, g1l, g2h, g2l, t12h, t12l,
    o1_ref, o2_ref, to_r_ref, to_l_ref, to_r2_ref, to_l2_ref, far_ref,
):
    comps, _, half = first_ref.shape
    quarter = half // 2

    def step(c, _):
        near = split(jnp.concatenate([l1_ref[c, :48], r1_ref[c, :48]], 0))
        rows = left(both(g1h, g1l), near)
        far_ref[c] = rows[112:]
        first = first_ref[c] + rows[:112]
        o1_ref[c] = first[:64]
        to_r_ref[c, :24] = first[64:88]
        to_l_ref[c, :24] = first[88:]
        return 0

    lax.fori_loop(0, comps, step, 0, unroll=True)
    far = right(split(far_ref[...].reshape(64 * comps, half)), both(t12h, t12l))
    for c in range(comps):
        deep = []
        for ref in (l1_ref, r1_ref):
            deep += [ref[c, 48:, :quarter], ref[c, 48:, quarter:]]
        for ref in (l2_ref, r2_ref):
            deep += [ref[c, :, :quarter], ref[c, :, quarter:]]
        second = left(both(g2h, g2l), split(jnp.concatenate(deep, 0)))
        second = second_ref[c] + (far[64 * c : 64 * c + 64] + second)
        o2_ref[c] = second[:16]
        for k, ref in enumerate((to_r_ref, to_l_ref)):
            ref[c, 24:, :quarter] = second[16 + 16 * k : 24 + 16 * k]
            ref[c, 24:, quarter:] = second[24 + 16 * k : 32 + 16 * k]
        to_r2_ref[c] = second[48:56]
        to_l2_ref[c] = second[56:]


def along_y_kernel(u_ref, b_ref):
    comps, lanes = u_ref.shape[:2]

    def step(n, _):
        c, k = n // lanes, n % lanes
        u, b = u_ref.at[c, k], b_ref.at[c, k]
        nothing = [jnp.zeros((8, 128), F32)] * 2
        for part in range(2):
            cells = [u[16 * y + 8 * part : 16 * y + 8 * part + 8] for y in range(ROWS)]
            for y, value in enumerate(lift_line(cells, nothing, nothing)):
                b[pl.ds(128 * part + y, 8, stride=ROWS)] = value
        return 0

    lax.fori_loop(0, comps * lanes, step, 0, unroll=4)


def rim_kernel(_, _2, own_ref, l_ref, r_ref, txh, txl, rims, b_ref, to_r_ref, to_l_ref, halo_ref, added_ref):
    comps, lanes = own_ref.shape[:2]
    blocks = lanes // 2

    def store(j, value):
        halo_ref[j] = value[:, :128]
        halo_ref[blocks + j] = value[:, 128:]

    rows = [ref[c, p] for c in range(comps) for ref in (l_ref, r_ref) for p in range(2)]
    lift_x(jnp.concatenate(rows, 0), both(txh, txl), rims, store)
    added_ref[...] = jnp.zeros_like(added_ref)
    units = np.eye(4)
    weights = np.array([lift_line([0.0] * ROWS, list(unit[:2]), list(unit[2:])) for unit in units])

    def step(n, _):
        c, k = n // lanes, n % lanes
        b, halo, added = b_ref.at[c, k], halo_ref.at[k], added_ref.at[n % 2]
        for part in range(2):
            around = [halo[pl.ds(pl.multiple_of(64 * c + 16 * p + 8 * part, 8), 8)] for p in range(4)]
            for y in range(ROWS):
                terms = [float(weights[p, y]) * around[p] for p in range(4) if weights[p, y] != 0.0]
                if terms:
                    added[pl.ds(128 * part + y, 8, stride=ROWS)] = sum(terms[1:], terms[0])
        for z in range(ROWS):
            at = slice(16 * z, 16 * z + 16)
            b[at] = own_ref[c, k, at] + added[at]

        def plane(z):
            return own_ref[c, k, 16 * z : 16 * z + 16] + added[16 * z : 16 * z + 16]

        to_r_ref[c, k, 0], to_r_ref[c, k, 1] = give_right([plane(z) for z in range(12, 16)])
        to_l_ref[c, k, 0], to_l_ref[c, k, 1] = give_left([plane(z) for z in range(3)])
        return 0

    lax.fori_loop(0, comps * lanes, step, 0, unroll=4)


def hand_on_kernel(_, value_ref, out_ref):
    out_ref[...] = value_ref[...]


def along_z_kernel(b_ref, l_ref, r_ref, out_ref, even_ref, done_ref, sems):
    comps, lanes = b_ref.shape[:2]

    def copy(c, k):
        return pltpu.make_async_copy(
            done_ref.at[c, k], out_ref.at[c, :, pl.ds(pl.multiple_of(128 * k, 128), 128)], sems.at[c]
        )

    def step(n, _):
        c, k = n // lanes, n % lanes
        b, done = b_ref.at[c, k], done_ref.at[c, k]
        for part in range(2):
            cells = [b[16 * z + 8 * part : 16 * z + 8 * part + 8] for z in range(ROWS)]
            around = [ref[c, k, p, 8 * part : 8 * part + 8] for ref in (l_ref, r_ref) for p in range(2)]
            for z, value in enumerate(lift_line(cells, around[:2], around[2:])):
                done[pl.ds(128 * part + z, 8, stride=ROWS)] = value
        copy(c, k).start()

        @pl.when(k < lanes // 2)
        def _():
            for y in range(ROWS // 2):
                even_ref[c, k, y] = done[32 * y : 32 * y + 16]

        return 0

    lax.fori_loop(0, comps * lanes, step, 0, unroll=4)
    for c in range(comps):
        for k in range(lanes):
            copy(c, k).wait()


def last_kernel(
    _, even_ref, o1_ref, o2_ref, l1_ref, r1_ref, l2_ref, r2_ref,
    g1h, g1l, g2h, g2l, t1h, t1l, out_ref, done_ref, sems,
):
    comps, lanes = even_ref.shape[:2]
    half = 128 * lanes
    quarter = half // 2
    window, deepest = [], []
    for c in range(comps):
        near = split(jnp.concatenate([l1_ref[c, :24], r1_ref[c, :24]], 0))
        window.append(o1_ref[c] + left(both(g1h, g1l), near))
        deep = []
        for ref in (l1_ref, r1_ref):
            deep += [ref[c, 24:, :quarter], ref[c, 24:, quarter:]]
        deep += [l2_ref[c], r2_ref[c]]
        deepest.append(o2_ref[c] + left(both(g2h, g2l), split(jnp.concatenate(deep, 0))))
    window = right(split(jnp.concatenate(window, 0)), both(t1h, t1l))
    copies = []
    for c in range(comps):
        for k in range(lanes):
            at = slice(128 * k, 128 * k + 128)
            for y in range(8):
                done_ref[c, k, y] = even_ref[c, k, y]
                done_ref[c, k, y, pl.ds(0, 8, stride=2)] = window[64 * c + 8 * y : 64 * c + 8 * y + 8, at]
            if 128 * k < quarter:
                for y in range(4):
                    done_ref[c, k, 2 * y, pl.ds(0, 4, stride=4)] = deepest[c][4 * y : 4 * y + 4, at]
            copies.append(pltpu.make_async_copy(done_ref.at[c, k], out_ref.at[c, :, 0, :, at], sems.at[c]))
            copies[-1].start()
    for copy in copies:
        copy.wait()


def call(body, ins, outs, scratch=(), flops=0, hbm_in=(), hbm_out=(), aliases=None):
    def spec(n, hbm):
        return pl.BlockSpec(memory_space=pltpu.HBM if n in hbm else pltpu.VMEM)

    moved = sum(a.size * a.dtype.itemsize for a in ins)
    moved += sum(int(np.prod(s)) * jnp.dtype(d).itemsize for s, d in outs)
    return pl.pallas_call(
        body,
        in_specs=[spec(n, hbm_in) for n in range(len(ins))],
        out_specs=[spec(n, hbm_out) for n in range(len(outs))],
        out_shape=[jax.ShapeDtypeStruct(s, d) for s, d in outs],
        scratch_shapes=list(scratch),
        input_output_aliases=aliases or {},
        compiler_params=pltpu.CompilerParams(vmem_limit_bytes=VMEM_LIMIT),
        cost_estimate=pl.CostEstimate(flops=flops, bytes_accessed=moved, transcendentals=0),
    )(*ins)


def move(value, axis, step):
    count = lax.axis_size(axis)
    return lax.ppermute(value, axis, [(i, (i + step) % count) for i in range(count)])


def local(flow_field):
    comps, ny, nz, nx = flow_field.shape
    assert ny == ROWS and nz == ROWS and nx % 1024 == 0
    assert lax.axis_size("gy") >= 5 and lax.axis_size("gz") >= 5
    half, quarter, lanes = nx // 2, nx // 4, nx // 128
    pairs = {k: [jnp.asarray(p) for p in v] for k, v in tables(nx).items()}
    field = pltpu.with_memory_space_constraint(flow_field, pltpu.HBM)
    flat = pltpu.with_memory_space_constraint(flow_field.reshape(comps, ROWS * ROWS, nx), pltpu.HBM)

    def consts(*names):
        return [p for n in names for p in pairs[n]]

    def dma(*shape):
        return pltpu.SemaphoreType.DMA(shape)

    edge = ((comps, 2, ROWS, nx), F32)
    y_right, y_left, head = call(
        edge_kernel,
        [field],
        [edge] * 2 + [((ROWS, ROWS, nx), F32)],
        [pltpu.VMEM((comps, 7, ROWS, nx), F32), dma(comps, 2), pltpu.SemaphoreType.DMA],
        hbm_in=(0,),
    )
    from_left0 = move(y_right, "gy", 1)
    from_right0 = move(y_left, "gy", -1)

    near = ((comps, 64, half), F32)
    far = ((comps, 16, half), F32)
    cells = ((comps, lanes, ROWS * ROWS, 128), F32)
    u, first, second, z_right, z_left, z_right2, z_left2 = call(
        lift_kernel,
        [flat, head.reshape(ROWS * ROWS, nx)] + consts("tx", "rims", "zsend", "tx12"),
        [cells, ((comps, 112, half), F32), ((comps, 64, quarter), F32)] + [near] * 2 + [far] * 2,
        [
            pltpu.VMEM((comps, ROWS * ROWS, nx), F32),
            pltpu.VMEM((ROWS * ROWS, half), BF16),
            pltpu.VMEM((ROWS * ROWS, half), BF16),
            pltpu.VMEM((comps, 192, half), F32),
            dma(comps),
        ],
        flops=1 << 33,
        hbm_in=(0,),
    )
    z_from_left2 = move(z_right2, "gz", 2)
    z_from_left = move(z_right, "gz", 1)
    z_from_right = move(z_left, "gz", -1)
    z_from_right2 = move(z_left2, "gz", -2)

    planes = ((comps, lanes, 2, ROWS, 128), F32)
    (own,) = call(along_y_kernel, [u], [cells], flops=1 << 31)
    b, z0_right, z0_left = call(
        rim_kernel,
        [z_from_left2, z_from_right2, own, from_left0, from_right0] + consts("tx", "rims"),
        [cells] + [planes] * 2,
        [pltpu.VMEM((lanes, 64 * comps, 128), F32), pltpu.VMEM((2, ROWS * ROWS, 128), F32)],
        flops=1 << 31,
    )
    z0_from_left = move(z0_right, "gz", 1)
    z0_from_right = move(z0_left, "gz", -1)

    o1, o2, y1_right, y1_left, y2_right, y2_left = call(
        chain_kernel,
        [first, second, z_from_left, z_from_right, z_from_left2, z_from_right2] + consts("chain1", "chain2", "tx12"),
        [((comps, 64, half), F32), ((comps, 16, quarter), F32)]
        + [((comps, 32, half), F32)] * 2
        + [((comps, 8, quarter), F32)] * 2,
        [pltpu.VMEM((comps, 64, half), F32)],
        flops=1 << 31,
    )
    y_from_left = move(y1_right, "gy", 1)
    y_from_left2 = move(y2_right, "gy", 2)
    (y1_left,) = call(hand_on_kernel, [z0_from_left, y1_left], [((comps, 32, half), F32)])
    (y2_left,) = call(hand_on_kernel, [z0_from_right, y2_left], [((comps, 8, quarter), F32)])
    y_from_right = move(y1_left, "gy", -1)
    y_from_right2 = move(y2_left, "gy", -2)

    whole = ((comps, ROWS * ROWS, nx), F32)
    result, even = call(
        along_z_kernel,
        [b, z0_from_left, z0_from_right],
        [whole, ((comps, lanes // 2, 8, ROWS, 128), F32)],
        [pltpu.VMEM((comps, lanes, ROWS * ROWS, 128), F32), dma(comps)],
        flops=1 << 32,
        hbm_out=(0,),
    )
    pairs_of_rows = ((comps, 8, 2, ROWS, nx), F32)
    (result,) = call(
        last_kernel,
        [result.reshape(pairs_of_rows[0]), even, o1, o2, y_from_left, y_from_right, y_from_left2, y_from_right2]
        + consts("ygive1", "ygive2", "tx1"),
        [pairs_of_rows],
        [pltpu.VMEM((comps, lanes // 2, 8, ROWS, 128), F32), dma(comps)],
        flops=1 << 30,
        hbm_in=(0,),
        hbm_out=(0,),
        aliases={0: 0},
    )
    return result.reshape(flow_field.shape)


def solution(mesh):
    placed = P(None, "gy", "gz", None)
    return jax.shard_map(local, mesh=mesh, in_specs=(placed,), out_specs=placed, check_vma=False)
```

```python
import jax
import jax.numpy as jnp
import ml_dtypes
import numpy as np
from jax import lax
from jax.experimental import pallas as pl
from jax.experimental.pallas import tpu as pltpu
from jax.sharding import PartitionSpec as P

ALPHA = -1.586134342059924
BETA = -0.052980118572961
GAMMA = 0.882911075530934
DELTA = 0.443506852043971
KAPPA = 1.149604398860241

F32 = jnp.float32
BF16 = jnp.bfloat16
VMEM_LIMIT = 32 * 1024 * 1024
ROWS = 16


def pair_matrix(length):
    cells = np.eye(length)
    even, odd = cells[0::2].copy(), cells[1::2].copy()
    odd = odd + ALPHA * (even + np.roll(even, -1, 0))
    even = even + BETA * (odd + np.roll(odd, 1, 0))
    odd = odd + GAMMA * (even + np.roll(even, -1, 0))
    even = even + DELTA * (odd + np.roll(odd, 1, 0))
    return even * KAPPA, odd / KAPPA


def alternated(length):
    low, high = pair_matrix(length)
    table = np.zeros((length, length))
    table[0::2], table[1::2] = low, high
    return table


def chain_blocks():
    count = 8
    length = count * ROWS
    first = alternated(length)
    second = alternated(length // 2) @ first[0::2]
    third = alternated(length // 4) @ second[0::2]
    result = []
    for table, per in ((first, 16), (second, 8), (third, 4)):
        here = table[4 * per : 5 * per]
        result.append({k: here[:, (4 + k) * ROWS : (5 + k) * ROWS] for k in (-2, -1, 0, 1, 2)})
    return result


def factor(block, rank):
    left, size, right = np.linalg.svd(block, full_matrices=False)
    assert np.all(size[rank:] < 1e-12)
    return left[:, :rank] * size[:rank], right[:rank]


def split_const(table):
    table = np.asarray(table, np.float64)
    high = table.astype(ml_dtypes.bfloat16)
    low = (table - high.astype(np.float64)).astype(ml_dtypes.bfloat16)
    return high, low


def stack(*parts):
    return np.concatenate(parts, 0)


def tables(nx):
    first, second, third = chain_blocks()
    eye = np.eye
    sides = (-1, 1)
    out = {}
    give1, send1, give2a, give2b, send2 = {}, {}, {}, {}, {}
    give2, send2d, give22, send22 = {}, {}, {}, {}
    for s in sides:
        give1[s], send1[s] = factor(second[s], 3)
        give2a[s] = third[s] @ send1[s].T
        give2b[s], send2[s] = factor(third[s] - give2a[s] @ send1[s], 2)
        give2[s], send2d[s] = factor(third[s], 4)
        give22[s], send22[s] = factor(third[2 * s], 2)

    low, high = pair_matrix(nx)
    out["tx"] = np.concatenate([low[128:256, 256:512], high[128:256, 256:512]], 0).T
    blocks = nx // 256
    rims = np.zeros((8 * blocks, nx))
    for j in range(blocks):
        block = np.concatenate([low[128 * j : 128 * j + 128], high[128 * j : 128 * j + 128]], 0).T
        after = (j + 1) % blocks
        rims[8 * j : 8 * j + 4, 256 * j : 256 * j + 256] = block[(256 * j - np.arange(4, 0, -1)) % nx]
        rims[8 * after + 4 : 8 * after + 8, 256 * j : 256 * j + 256] = block[256 * after : 256 * after + 4]
    low, high = pair_matrix(nx // 2)
    tx1 = np.concatenate([low, high], 0).T
    low, high = pair_matrix(nx // 4)
    tx2 = np.concatenate([low, high], 0).T
    out["tx1"] = tx1
    out["tx12"] = tx1[:, : nx // 4] @ tx2

    def planes(send):
        return np.einsum("pz,ab->paBz".replace("B", "b"), send, eye(ROWS)).reshape(-1, ROWS * ROWS)

    zsend = [planes(send[s]) for send in (send1, send2, send22) for s in sides]

    def back(give):
        return np.einsum("zp,ab->azpb", give, eye(ROWS)).reshape(ROWS * give.shape[0], -1)

    zgive1 = np.concatenate([back(give1[s]) for s in sides], 1)
    zgive2a = np.concatenate([back(give2a[s]) for s in sides], 1)
    zgive2b = np.concatenate([back(give2b[s]) for s in sides] + [back(give22[s]) for s in sides], 1)
    ychain1 = stack(np.kron(second[0], eye(8)), *[np.kron(send1[s], eye(8)) for s in sides])
    ychain2 = stack(
        np.kron(third[0], eye(4)),
        *[np.kron(send2d[s], eye(4)) for s in sides],
        *[np.kron(send22[s], eye(4)) for s in sides],
    )
    own1, own2 = np.kron(eye(ROWS), second[0]), np.kron(eye(ROWS), third[0])
    out["zsend"] = stack(*zsend, ychain2 @ own2, ychain1 @ own1)
    out["chain1"] = stack(ychain1 @ zgive1, ychain2 @ zgive2a)
    out["chain2"] = ychain2 @ zgive2b
    out["ygive1"] = np.concatenate([np.kron(give1[s], eye(8)) for s in sides], 1)
    out["ygive2"] = np.concatenate(
        [np.kron(give2[s], eye(4)) for s in sides] + [np.kron(give22[s], eye(4)) for s in sides], 1
    )
    pairs = {name: split_const(table) for name, table in out.items()}
    high, low = split_const(rims)
    pairs["rims"] = (np.concatenate([high, high, low, np.zeros_like(high)], 0),)
    return pairs


def split(value):
    high = value.astype(BF16)
    low = (value - high.astype(F32)).astype(BF16)
    return high, low


def dot(a, b):
    return jnp.dot(a, b, preferred_element_type=F32)


def left(table, rows):
    return dot(table[0], rows[0]) + (dot(table[0], rows[1]) + dot(table[1], rows[0]))


def right(rows, table):
    return dot(rows[0], table[0]) + (dot(rows[0], table[1]) + dot(rows[1], table[0]))


def both(high_ref, low_ref):
    return high_ref[...], low_ref[...]


def lift_line(cells, before, after):
    even, odd = list(cells[0::2]), list(cells[1::2])
    count = len(even)
    even.append(after[0])
    odd = [odd[n] + ALPHA * (even[n] + even[n + 1]) for n in range(count)]
    odd_before = before[0] + ALPHA * even[0]
    even_before = before[1] + BETA * odd_before
    odd_around = [odd_before] + odd + [after[1]]
    even = [even[n] + BETA * (odd_around[n + 1] + odd_around[n]) for n in range(count + 1)]
    odd = [odd[n] + GAMMA * (even[n] + even[n + 1]) for n in range(count)]
    odd_around = [odd_before + GAMMA * (even_before + even[0])] + odd
    even = [even[n] + DELTA * (odd_around[n + 1] + odd_around[n]) for n in range(count)]
    result = []
    for n in range(count):
        result += [even[n] * KAPPA, odd[n] * (1.0 / KAPPA)]
    return result


def give_right(cells):
    a, b, c, d = cells
    return d + ALPHA * c, c + BETA * (b + ALPHA * (a + c))


def give_left(cells):
    a, b, c = cells
    return a, b + ALPHA * (a + c)


def lift_x(cells, table, rims_ref, store):
    count, nx = cells.shape
    lane = lax.broadcasted_iota(jnp.int32, (count, 128), 1)
    rims = None
    for j in range(nx // 256):
        at = 256 * j
        before = cells[:, nx - 128 :] if j == 0 else cells[:, at - 128 : at]
        rim = jnp.where(lane >= 124, before, jnp.where(lane < 4, cells[:, at : at + 128], 0.0))
        rim = pltpu.roll(rim, 4 + 8 * j, 1)
        rims = rim if rims is None else rims + rim
    width = nx // 32
    high = rims.astype(BF16).astype(F32)
    rims = (high + pltpu.roll(rims - high, width, 1) + pltpu.roll(high, 2 * width, 1)).astype(BF16)
    parts = split(cells)
    for j in range(nx // 256):
        lanes = slice(256 * j, 256 * j + 256)
        store(j, right([part[:, lanes] for part in parts], table) + dot(rims, rims_ref[:, lanes]))


def edge_kernel(x_ref, to_right_ref, to_left_ref, head_ref, rows_ref, sems, head_sem):
    comps = x_ref.shape[0]
    copies = []
    for c in range(comps):
        copies.append(pltpu.make_async_copy(x_ref.at[c, pl.ds(0, 3)], rows_ref.at[c, pl.ds(0, 3)], sems.at[c, 0]))
        copies.append(pltpu.make_async_copy(x_ref.at[c, pl.ds(12, 4)], rows_ref.at[c, pl.ds(3, 4)], sems.at[c, 1]))
    head = pltpu.make_async_copy(x_ref.at[0], head_ref, head_sem)
    for copy in copies:
        copy.start()
    head.start()
    for c in range(comps):
        copies[2 * c].wait()
        to_left_ref[c, 0], to_left_ref[c, 1] = give_left([rows_ref[c, k] for k in range(3)])
        copies[2 * c + 1].wait()
        to_right_ref[c, 0], to_right_ref[c, 1] = give_right([rows_ref[c, k] for k in range(3, 7)])
    head.wait()


def lift_kernel(
    x_ref, head_ref, txh, txl, rims, zsh, zsl, t12h, t12l,
    u_ref, first_ref, second_ref, r1_ref, l1_ref, r2_ref, l2_ref, cells_ref, high_ref, low_ref, far_ref, sems,
):
    comps, _, nx = x_ref.shape
    blocks, quarter = nx // 256, nx // 4

    def copy(c):
        return pltpu.make_async_copy(x_ref.at[c], cells_ref.at[c], sems.at[c])

    for c in range(1, comps):
        copy(c).start()

    def part(c, cells):
        def store(j, value):
            u_ref[c, j] = value[:, :128]
            u_ref[c, blocks + j] = value[:, 128:]
            high, low = split(value[:, :128])
            high_ref[:, 128 * j : 128 * j + 128] = high
            low_ref[:, 128 * j : 128 * j + 128] = low

        lift_x(cells, both(txh, txl), rims, store)
        rows = left(both(zsh, zsl), both(high_ref, low_ref))
        r1_ref[c, :48] = rows[:48]
        l1_ref[c, :48] = rows[48:96]
        far_ref[c] = rows[96:288]
        first_ref[c] = rows[288:]

    def step(c, _):
        copy(c).wait()
        part(c, cells_ref[c])
        return 0

    part(0, head_ref[...])
    lax.fori_loop(1, comps, step, 0, unroll=True)
    far = right(split(far_ref[...].reshape(192 * comps, nx // 2)), both(t12h, t12l))
    for c in range(comps):
        for k, (ref, ref2) in enumerate(((r1_ref, r2_ref), (l1_ref, l2_ref))):
            for p in range(2):
                lanes = slice(quarter * p, quarter * p + quarter)
                at = 192 * c + 32 * k + 16 * p
                ref[c, 48:, lanes] = far[at : at + 16]
                ref2[c, :, lanes] = far[at + 64 : at + 80]
        second_ref[c] = far[192 * c + 128 : 192 * c + 192]


def chain_kernel(
    first_ref, second_ref, l1_ref, r1_ref, l2_ref, r2_ref,
    g1h, g1l, g2h, g2l, t12h, t12l,
    o1_ref, o2_ref, to_r_ref, to_l_ref, to_r2_ref, to_l2_ref, far_ref,
):
    comps, _, half = first_ref.shape
    quarter = half // 2

    def step(c, _):
        near = split(jnp.concatenate([l1_ref[c, :48], r1_ref[c, :48]], 0))
        rows = left(both(g1h, g1l), near)
        far_ref[c] = rows[112:]
        first = first_ref[c] + rows[:112]
        o1_ref[c] = first[:64]
        to_r_ref[c, :24] = first[64:88]
        to_l_ref[c, :24] = first[88:]
        return 0

    lax.fori_loop(0, comps, step, 0, unroll=True)
    far = right(split(far_ref[...].reshape(64 * comps, half)), both(t12h, t12l))
    for c in range(comps):
        deep = []
        for ref in (l1_ref, r1_ref):
            deep += [ref[c, 48:, :quarter], ref[c, 48:, quarter:]]
        for ref in (l2_ref, r2_ref):
            deep += [ref[c, :, :quarter], ref[c, :, quarter:]]
        second = left(both(g2h, g2l), split(jnp.concatenate(deep, 0)))
        second = second_ref[c] + (far[64 * c : 64 * c + 64] + second)
        o2_ref[c] = second[:16]
        for k, ref in enumerate((to_r_ref, to_l_ref)):
            ref[c, 24:, :quarter] = second[16 + 16 * k : 24 + 16 * k]
            ref[c, 24:, quarter:] = second[24 + 16 * k : 32 + 16 * k]
        to_r2_ref[c] = second[48:56]
        to_l2_ref[c] = second[56:]


def along_y_kernel(u_ref, b_ref):
    comps, lanes = u_ref.shape[:2]

    def step(n, _):
        c, k = n // lanes, n % lanes
        u, b = u_ref.at[c, k], b_ref.at[c, k]
        nothing = [jnp.zeros((8, 128), F32)] * 2
        for part in range(2):
            cells = [u[16 * y + 8 * part : 16 * y + 8 * part + 8] for y in range(ROWS)]
            for y, value in enumerate(lift_line(cells, nothing, nothing)):
                b[pl.ds(128 * part + y, 8, stride=ROWS)] = value
        return 0

    lax.fori_loop(0, comps * lanes, step, 0, unroll=4)


def rim_kernel(_, _2, own_ref, l_ref, r_ref, txh, txl, rims, b_ref, to_r_ref, to_l_ref, halo_ref, added_ref):
    comps, lanes = own_ref.shape[:2]
    blocks = lanes // 2

    def store(j, value):
        halo_ref[j] = value[:, :128]
        halo_ref[blocks + j] = value[:, 128:]

    rows = [ref[c, p] for c in range(comps) for ref in (l_ref, r_ref) for p in range(2)]
    lift_x(jnp.concatenate(rows, 0), both(txh, txl), rims, store)
    added_ref[...] = jnp.zeros_like(added_ref)
    units = np.eye(4)
    weights = np.array([lift_line([0.0] * ROWS, list(unit[:2]), list(unit[2:])) for unit in units])

    def step(n, _):
        c, k = n // lanes, n % lanes
        b, halo, added = b_ref.at[c, k], halo_ref.at[k], added_ref.at[n % 2]
        for part in range(2):
            around = [halo[pl.ds(pl.multiple_of(64 * c + 16 * p + 8 * part, 8), 8)] for p in range(4)]
            for y in range(ROWS):
                terms = [float(weights[p, y]) * around[p] for p in range(4) if weights[p, y] != 0.0]
                if terms:
                    added[pl.ds(128 * part + y, 8, stride=ROWS)] = sum(terms[1:], terms[0])
        for z in range(ROWS):
            at = slice(16 * z, 16 * z + 16)
            b[at] = own_ref[c, k, at] + added[at]

        def plane(z):
            return own_ref[c, k, 16 * z : 16 * z + 16] + added[16 * z : 16 * z + 16]

        to_r_ref[c, k, 0], to_r_ref[c, k, 1] = give_right([plane(z) for z in range(12, 16)])
        to_l_ref[c, k, 0], to_l_ref[c, k, 1] = give_left([plane(z) for z in range(3)])
        return 0

    lax.fori_loop(0, comps * lanes, step, 0, unroll=4)


def hand_on_kernel(_, value_ref, out_ref):
    out_ref[...] = value_ref[...]


def along_z_kernel(b_ref, l_ref, r_ref, out_ref, even_ref, done_ref, sems):
    comps, lanes = b_ref.shape[:2]

    def copy(c, k):
        return pltpu.make_async_copy(
            done_ref.at[c, k], out_ref.at[c, :, pl.ds(pl.multiple_of(128 * k, 128), 128)], sems.at[c]
        )

    def step(n, _):
        c, k = n // lanes, n % lanes
        b, done = b_ref.at[c, k], done_ref.at[c, k]
        for part in range(2):
            cells = [b[16 * z + 8 * part : 16 * z + 8 * part + 8] for z in range(ROWS)]
            around = [ref[c, k, p, 8 * part : 8 * part + 8] for ref in (l_ref, r_ref) for p in range(2)]
            for z, value in enumerate(lift_line(cells, around[:2], around[2:])):
                done[pl.ds(128 * part + z, 8, stride=ROWS)] = value
        copy(c, k).start()

        @pl.when(k < lanes // 2)
        def _():
            for y in range(ROWS // 2):
                even_ref[c, k, y] = done[32 * y : 32 * y + 16]

        return 0

    lax.fori_loop(0, comps * lanes, step, 0, unroll=4)
    for c in range(comps):
        for k in range(lanes):
            copy(c, k).wait()


def last_kernel(
    _, even_ref, o1_ref, o2_ref, l1_ref, r1_ref, l2_ref, r2_ref,
    g1h, g1l, g2h, g2l, t1h, t1l, out_ref, done_ref, sems,
):
    comps, lanes = even_ref.shape[:2]
    half = 128 * lanes
    quarter = half // 2
    window, deepest = [], []
    for c in range(comps):
        near = split(jnp.concatenate([l1_ref[c, :24], r1_ref[c, :24]], 0))
        window.append(o1_ref[c] + left(both(g1h, g1l), near))
        deep = []
        for ref in (l1_ref, r1_ref):
            deep += [ref[c, 24:, :quarter], ref[c, 24:, quarter:]]
        deep += [l2_ref[c], r2_ref[c]]
        deepest.append(o2_ref[c] + left(both(g2h, g2l), split(jnp.concatenate(deep, 0))))
    window = right(split(jnp.concatenate(window, 0)), both(t1h, t1l))
    copies = []
    for c in range(comps):
        for k in range(lanes):
            at = slice(128 * k, 128 * k + 128)
            for y in range(8):
                done_ref[c, k, y] = even_ref[c, k, y]
                done_ref[c, k, y, pl.ds(0, 8, stride=2)] = window[64 * c + 8 * y : 64 * c + 8 * y + 8, at]
            if 128 * k < quarter:
                for y in range(4):
                    done_ref[c, k, 2 * y, pl.ds(0, 4, stride=4)] = deepest[c][4 * y : 4 * y + 4, at]
            copies.append(pltpu.make_async_copy(done_ref.at[c, k], out_ref.at[c, :, 0, :, at], sems.at[c]))
            copies[-1].start()
    for copy in copies:
        copy.wait()


def call(body, ins, outs, scratch=(), flops=0, hbm_in=(), hbm_out=(), aliases=None):
    def spec(n, hbm):
        return pl.BlockSpec(memory_space=pltpu.HBM if n in hbm else pltpu.VMEM)

    moved = sum(a.size * a.dtype.itemsize for a in ins)
    moved += sum(int(np.prod(s)) * jnp.dtype(d).itemsize for s, d in outs)
    return pl.pallas_call(
        body,
        in_specs=[spec(n, hbm_in) for n in range(len(ins))],
        out_specs=[spec(n, hbm_out) for n in range(len(outs))],
        out_shape=[jax.ShapeDtypeStruct(s, d) for s, d in outs],
        scratch_shapes=list(scratch),
        input_output_aliases=aliases or {},
        compiler_params=pltpu.CompilerParams(vmem_limit_bytes=VMEM_LIMIT),
        cost_estimate=pl.CostEstimate(flops=flops, bytes_accessed=moved, transcendentals=0),
    )(*ins)


def move(value, axis, step):
    count = lax.axis_size(axis)
    return lax.ppermute(value, axis, [(i, (i + step) % count) for i in range(count)])


def local(flow_field):
    comps, ny, nz, nx = flow_field.shape
    assert ny == ROWS and nz == ROWS and nx % 1024 == 0
    assert lax.axis_size("gy") >= 5 and lax.axis_size("gz") >= 5
    half, quarter, lanes = nx // 2, nx // 4, nx // 128
    pairs = {k: [jnp.asarray(p) for p in v] for k, v in tables(nx).items()}
    field = pltpu.with_memory_space_constraint(flow_field, pltpu.HBM)
    flat = pltpu.with_memory_space_constraint(flow_field.reshape(comps, ROWS * ROWS, nx), pltpu.HBM)

    def consts(*names):
        return [p for n in names for p in pairs[n]]

    def dma(*shape):
        return pltpu.SemaphoreType.DMA(shape)

    edge = ((comps, 2, ROWS, nx), F32)
    y_right, y_left, head = call(
        edge_kernel,
        [field],
        [edge] * 2 + [((ROWS, ROWS, nx), F32)],
        [pltpu.VMEM((comps, 7, ROWS, nx), F32), dma(comps, 2), pltpu.SemaphoreType.DMA],
        hbm_in=(0,),
    )
    from_left0 = move(y_right, "gy", 1)
    from_right0 = move(y_left, "gy", -1)

    near = ((comps, 64, half), F32)
    far = ((comps, 16, half), F32)
    cells = ((comps, lanes, ROWS * ROWS, 128), F32)
    u, first, second, z_right, z_left, z_right2, z_left2 = call(
        lift_kernel,
        [flat, head.reshape(ROWS * ROWS, nx)] + consts("tx", "rims", "zsend", "tx12"),
        [cells, ((comps, 112, half), F32), ((comps, 64, quarter), F32)] + [near] * 2 + [far] * 2,
        [
            pltpu.VMEM((comps, ROWS * ROWS, nx), F32),
            pltpu.VMEM((ROWS * ROWS, half), BF16),
            pltpu.VMEM((ROWS * ROWS, half), BF16),
            pltpu.VMEM((comps, 192, half), F32),
            dma(comps),
        ],
        flops=1 << 33,
        hbm_in=(0,),
    )
    z_from_left2 = move(z_right2, "gz", 2)
    z_from_left = move(z_right, "gz", 1)
    z_from_right = move(z_left, "gz", -1)
    z_from_right2 = move(z_left2, "gz", -2)

    planes = ((comps, lanes, 2, ROWS, 128), F32)
    (own,) = call(along_y_kernel, [u], [cells], flops=1 << 31)
    b, z0_right, z0_left = call(
        rim_kernel,
        [z_from_left2, z_from_right2, own, from_left0, from_right0] + consts("tx", "rims"),
        [cells] + [planes] * 2,
        [pltpu.VMEM((lanes, 64 * comps, 128), F32), pltpu.VMEM((2, ROWS * ROWS, 128), F32)],
        flops=1 << 31,
    )
    z0_from_left = move(z0_right, "gz", 1)
    z0_from_right = move(z0_left, "gz", -1)

    o1, o2, y1_right, y1_left, y2_right, y2_left = call(
        chain_kernel,
        [first, second, z_from_left, z_from_right, z_from_left2, z_from_right2] + consts("chain1", "chain2", "tx12"),
        [((comps, 64, half), F32), ((comps, 16, quarter), F32)]
        + [((comps, 32, half), F32)] * 2
        + [((comps, 8, quarter), F32)] * 2,
        [pltpu.VMEM((comps, 64, half), F32)],
        flops=1 << 31,
    )
    y_from_right = move(y1_left, "gy", -1)
    y_from_right2 = move(y2_left, "gy", -2)
    (y1_right,) = call(hand_on_kernel, [z0_from_left, y1_right], [((comps, 32, half), F32)])
    (y2_right,) = call(hand_on_kernel, [z0_from_right, y2_right], [((comps, 8, quarter), F32)])
    y_from_left = move(y1_right, "gy", 1)
    y_from_left2 = move(y2_right, "gy", 2)

    whole = ((comps, ROWS * ROWS, nx), F32)
    result, even = call(
        along_z_kernel,
        [b, z0_from_left, z0_from_right],
        [whole, ((comps, lanes // 2, 8, ROWS, 128), F32)],
        [pltpu.VMEM((comps, lanes, ROWS * ROWS, 128), F32), dma(comps)],
        flops=1 << 32,
        hbm_out=(0,),
    )
    pairs_of_rows = ((comps, 8, 2, ROWS, nx), F32)
    (result,) = call(
        last_kernel,
        [result.reshape(pairs_of_rows[0]), even, o1, o2, y_from_left, y_from_right, y_from_left2, y_from_right2]
        + consts("ygive1", "ygive2", "tx1"),
        [pairs_of_rows],
        [pltpu.VMEM((comps, lanes // 2, 8, ROWS, 128), F32), dma(comps)],
        flops=1 << 30,
        hbm_in=(0,),
        hbm_out=(0,),
        aliases={0: 0},
    )
    return result.reshape(flow_field.shape)


def solution(mesh):
    placed = P(None, "gy", "gz", None)
    return jax.shard_map(local, mesh=mesh, in_specs=(placed,), out_specs=placed, check_vma=False)
```
